256 devices in a mesh: replica: 64 (over z_lo, x, y), tensor: 4 (over z_hi, core).
Axes of the slice: x: 4, y: 4, z: 8 (z_hi: 2, z_lo: 4; z = z_hi * 4 + z_lo), core: 2. Of those that a mesh axis runs over, the one named last changes fastest.
Arguments:
- hidden: bfloat16 [128, 4096], P('replica'), may hold values from -6 to 6
- queries: bfloat16 [128, 2048], P('replica', 'tensor'), may hold values from -1.73 to 1.73
- new_key: bfloat16 [128, 2048], P('replica', 'tensor'), may hold values from -6 to 6
- new_value: bfloat16 [128, 2048], P('replica', 'tensor'), may hold values from -6 to 6
- cache_keys: bfloat16 [128, 768, 2048], P('replica', None, 'tensor'), may hold values from -35 to 35
- cache_values: bfloat16 [128, 768, 2048], P('replica', None, 'tensor'), may hold values from -6 to 6
- w_out: bfloat16 [2048, 4096], P('tensor'), may hold values from -0.5 to 0.5
- lengths: int32 [128], replicated, may hold values from 16 to 767
- moved_slot: int32 [64], replicated, may hold values from -1 to 1, as said below
Outputs:
- layer_out: bfloat16 [128, 4096], P('replica', 'tensor')
- keys_out: bfloat16 [128, 768, 2048], P('replica', None, 'tensor')
- values_out: bfloat16 [128, 768, 2048], P('replica', None, 'tensor')
The draws below stay inside these ranges and needn't reach their ends.
Inputs may be any that keep to these rules, and one draw needn't show every extreme that they name: moved_slot[r] is -1 exactly when moved_slot[(r + 32) mod 64] is -1.
All inputs are finite; a program needn't handle non-finite values.
Results may differ from the reference program's by a relative error of at most 0.0053.
Values may be sent and summed in bfloat16 or wider, within the bound.
A program may use at most 64 MiB of HBM per device.

```python
import jax
import jax.numpy as jnp
from jax import lax

D = 4096
HEADS = 16
HEAD_DIM = 128
SLOT_DEV = 2
CAP = 768
SLOTS = 128
N_REPLICA = 64


def query_field(key):
    return jax.random.uniform(jax.random.fold_in(key, 7), (SLOTS, HEADS * HEAD_DIM), jnp.float32, -1.73, 1.73)


def heavy_flags(key):
    return jax.random.randint(jax.random.fold_in(key, 21), (N_REPLICA,), 0, 2)


def draw_queries(key, part):
    shared = query_field(key)
    return shared.astype(jnp.bfloat16)


def draw_cache_keys(key, part):
    key = jax.random.fold_in(key, 11)
    drawn = jax.random.uniform(key, (SLOTS, CAP, HEADS * HEAD_DIM), jnp.float32, -1.73, 1.73)
    return drawn.astype(jnp.bfloat16)


def draw_lengths(key, part):
    heavy_flag = heavy_flags(key)
    key = jax.random.fold_in(key, 5)
    long_key, short_key = jax.random.split(key, 2)
    long_len = jax.random.randint(long_key, (SLOTS,), CAP // 2, 3 * CAP // 4)
    short_len = jax.random.randint(short_key, (SLOTS,), 16, max(17, CAP // 4))
    heavy_slot = jnp.repeat(heavy_flag, SLOT_DEV)
    result = jnp.where(heavy_slot == 1, long_len, short_len)
    result = result.at[SLOT_DEV].set(CAP - 1)
    result = result.at[(SLOT_DEV + 1) % SLOTS].set(16)
    return result.astype(jnp.int32)


def draw_moved_slot(key, part):
    heavy_flag = heavy_flags(key)
    key = jax.random.fold_in(key, 9)
    low_key, high_key = jax.random.split(key, 2)
    half_count = N_REPLICA // 2
    moving = (heavy_flag[:half_count] != heavy_flag[half_count:]).astype(jnp.int32)
    moving = moving.at[0].set(1).at[1].set(0)
    lower_side = jax.random.randint(low_key, (half_count,), 0, SLOT_DEV).at[0].set(SLOT_DEV - 1)
    upper_side = jax.random.randint(high_key, (half_count,), 0, SLOT_DEV)
    lower_side = jnp.where(moving == 1, lower_side, -1)
    upper_side = jnp.where(moving == 1, upper_side, -1)
    return jnp.concatenate([lower_side, upper_side]).astype(jnp.int32)


def level_of(own_key, extent, cuts, least, top_value):
    def one(dim, shards_of):
        steps = jax.random.uniform(jax.random.fold_in(jax.random.fold_in(own_key, 6), dim), (shards_of,), jnp.float32, least / len(cuts), top_value / len(cuts))
        return jnp.repeat(jnp.exp(steps), extent[dim] // shards_of).reshape((-1,) + (1,) * (len(extent) - dim - 1))

    loudness = one(*cuts[0])
    for cut in cuts[1:]:
        loudness = loudness * one(*cut)
    return loudness


def centred(key, dims, width, limit, cuts=(), kind=jnp.bfloat16):
    values = width * jax.random.normal(key, dims, jnp.float32)
    if cuts:
        values = values * level_of(key, dims, cuts, -0.22, 0.18)
    return jnp.clip(values, -limit, limit).astype(kind)


def setup_inputs(seed: int = 0) -> dict:
    streams_of = jax.random.split(jax.random.key(seed), 10)
    hidden = centred(streams_of[0], (SLOTS, D), 1.0, 6.0, ((0, 64),))
    queries = draw_queries(jax.random.fold_in(streams_of[9], 71), 0)
    new_key = centred(streams_of[2], (SLOTS, HEADS * HEAD_DIM), 1.0, 6.0, ((0, 64), (1, 4)))
    new_value = centred(streams_of[3], (SLOTS, HEADS * HEAD_DIM), 1.0, 6.0, ((0, 64), (1, 4)))
    cache_keys = draw_cache_keys(jax.random.fold_in(streams_of[9], 71), 0)
    cache_values = centred(streams_of[5], (SLOTS, CAP, HEADS * HEAD_DIM), 1.0, 6.0, ((0, 64), (2, 4)))
    w_out = centred(streams_of[6], (HEADS * HEAD_DIM, D), HEAD_DIM ** -0.5, 0.5, ((0, 4),))
    lengths = draw_lengths(jax.random.fold_in(streams_of[9], 71), 0)
    moved_slot = draw_moved_slot(jax.random.fold_in(streams_of[9], 71), 0)
    return {"hidden": hidden, "queries": queries, "new_key": new_key, "new_value": new_value, "cache_keys": cache_keys, "cache_values": cache_values, "w_out": w_out, "lengths": lengths, "moved_slot": moved_slot}


def appended(cache_row, fresh, length, positions):
    return jnp.where(positions[:, None] < length, cache_row, jnp.where(positions[:, None] == length, fresh[None, :], jnp.zeros_like(cache_row)))


def reference(hidden, queries, new_key, new_value, cache_keys, cache_values, w_out, lengths, moved_slot):
    slot_ids = jnp.arange(SLOTS, dtype=jnp.int32)
    replica_ids = slot_ids // SLOT_DEV
    within = slot_ids % SLOT_DEV
    partner_ids = (replica_ids + N_REPLICA // 2) % N_REPLICA
    leaving = moved_slot[replica_ids]
    sources = jnp.where(leaving == within, partner_ids * SLOT_DEV + moved_slot[partner_ids], slot_ids).astype(jnp.int32)
    positions = jnp.arange(CAP, dtype=jnp.int32)

    def one_row(source_slot):
        length = lengths[source_slot]
        key_rows = appended(cache_keys[source_slot], new_key[source_slot], length, positions)
        value_rows = appended(cache_values[source_slot], new_value[source_slot], length, positions)
        q_split = queries[source_slot].astype(jnp.float32).reshape(HEADS, HEAD_DIM)
        k_split = key_rows.astype(jnp.float32).reshape(CAP, HEADS, HEAD_DIM)
        v_split = value_rows.astype(jnp.float32).reshape(CAP, HEADS, HEAD_DIM)
        scores = jnp.einsum("hd,chd->hc", q_split, k_split, precision=lax.Precision.HIGHEST) * (HEAD_DIM ** -0.5)
        scores = jnp.where(positions[None, :] <= length, scores, -1e30)
        peak_score = jnp.max(scores, axis=1, keepdims=True)
        exp_terms = jnp.exp(scores - peak_score)
        weights = (exp_terms / jnp.sum(exp_terms, axis=1, keepdims=True)).astype(jnp.bfloat16)
        attended = jnp.einsum("hc,chd->hd", weights.astype(jnp.float32), v_split, precision=lax.Precision.HIGHEST)
        attended = attended.reshape(HEADS * HEAD_DIM).astype(jnp.bfloat16)
        branch = jnp.dot(attended[None, :], w_out, preferred_element_type=jnp.float32)[0]
        layer_row = (hidden[source_slot].astype(jnp.float32) + branch).astype(jnp.bfloat16)
        return layer_row, key_rows, value_rows

    layer_out, keys_out, values_out = lax.map(one_row, sources)
    return layer_out, keys_out, values_out
```

```python
import functools

import jax
import jax.numpy as jnp
from jax import lax
from jax.experimental import pallas as pl
from jax.experimental.pallas import tpu as pltpu
from jax.sharding import PartitionSpec as P

HEAD_DIM = 128
TILE = 16
LANES = 256
MESH = pl.DeviceIdType.MESH


def block_diagonal(row, heads):
    width = row.shape[1]
    row_id = lax.broadcasted_iota(jnp.int32, (8, width), 0)
    col_id = lax.broadcasted_iota(jnp.int32, (8, width), 1)
    own = (col_id >= row_id * HEAD_DIM) & (col_id < row_id * HEAD_DIM + HEAD_DIM)
    return own, jnp.where(own, jnp.broadcast_to(row, (8, width)), 0.0)


def attend_row(query, fresh_key, fresh_value, keys_ref, values_ref, length):
    cap, width = keys_ref.shape
    own, query_block = block_diagonal(query, width // HEAD_DIM)
    scale = HEAD_DIM**-0.5
    scores = lax.dot_general(
        query_block.astype(jnp.bfloat16), keys_ref[...], (((1,), (1,)), ((), ())), preferred_element_type=jnp.float32
    )
    scores = scores * scale
    fresh_score = jnp.sum(query_block * fresh_key, axis=1, keepdims=True) * scale
    position = lax.broadcasted_iota(jnp.int32, scores.shape, 1)
    live = position < length
    peak = jnp.maximum(jnp.max(jnp.where(live, scores, -1e30), axis=1, keepdims=True), fresh_score)
    terms = jnp.where(live, jnp.exp(jnp.minimum(scores - peak, 0.0)), 0.0)
    fresh_term = jnp.exp(fresh_score - peak)
    total = jnp.sum(terms, axis=1, keepdims=True) + fresh_term
    weights = (terms / total).astype(jnp.bfloat16)
    fresh_weight = (fresh_term / total).astype(jnp.bfloat16).astype(jnp.float32)
    mixed = lax.dot_general(
        weights, values_ref[...], (((1,), (0,)), ((), ())), preferred_element_type=jnp.float32
    )
    mixed = mixed + fresh_weight * fresh_value
    return jnp.sum(jnp.where(own, mixed, 0.0), axis=0, keepdims=True)


def as_rows(two_rows):
    pieces = [two_rows[s : s + 1, j * 128 : (j + 1) * 128] for s in range(2) for j in range(8)]
    return jnp.concatenate(pieces, axis=0)


def as_line(rows):
    return jnp.concatenate([rows[j : j + 1, :] for j in range(8)], axis=1)


def move_kernel(
    depth,
    lengths, moved, hidden, queries, new_key, new_value, cache_keys, cache_values, w_out,
    layer_out, arrived,
    keys, values, weights, outgoing, partial, partial_in,
    load_sem, weight_sem, move_send, move_recv, part_send, part_recv,
):
    replica = lax.axis_index("replica")
    tensor = lax.axis_index("tensor")
    partner = (replica + 32) % 64

    loads = []
    for kind, (source, held) in enumerate(((cache_keys, keys), (cache_values, values))):
        load = pltpu.make_async_copy(source, held, load_sem.at[kind])
        load.start()
        loads.append(load)
    weight_load = pltpu.make_async_copy(w_out, weights, weight_sem)
    weight_load.start()

    peers = [(replica, (tensor + k) % 4) for k in range(1, 4)]
    peers += [(partner, (tensor + k) % 4) for k in range(4)]
    barrier = pltpu.get_barrier_semaphore()
    for peer in peers:
        pl.semaphore_signal(barrier, inc=1, device_id=peer, device_id_type=MESH)

    leaving = moved[replica]
    leaving_slot = jnp.maximum(leaving, 0)
    leaving_length = lengths[replica * 2 + leaving_slot]
    key_rows = new_key[...].astype(jnp.float32)
    value_rows = new_value[...].astype(jnp.float32)
    in_tile = lax.broadcasted_iota(jnp.int32, (TILE, LANES), 0)

    moves = []
    for quarter in range(4):
        kind, half = quarter // 2, quarter % 2
        held = (keys, values)[kind]
        fresh_rows = (key_rows, value_rows)[kind][:, half * LANES : (half + 1) * LANES]
        fresh = jnp.where(leaving_slot == 1, fresh_rows[1:2], fresh_rows[0:1])
        fresh = jnp.broadcast_to(fresh, (TILE, LANES))
        if half == 0:
            loads[kind].wait()

        def pack(step, carry, held=held, half=half, quarter=quarter, fresh=fresh):
            for j in range(4):
                block = step * 4 + j
                tile = held[leaving_slot, pl.ds(block * TILE, TILE), half * LANES : (half + 1) * LANES]
                position = in_tile + block * TILE
                tile = jnp.where(position < leaving_length, tile.astype(jnp.float32), fresh)
                outgoing[quarter * 4 + j, step] = tile.astype(jnp.bfloat16)
            return carry

        lax.fori_loop(0, depth, pack, 0)
        if quarter == 0:
            pl.semaphore_wait(barrier, len(peers))
        move = pltpu.make_async_remote_copy(
            src_ref=outgoing.at[quarter * 4 : quarter * 4 + 4, 0:depth],
            dst_ref=arrived.at[quarter * 4 : quarter * 4 + 4, 0:depth],
            send_sem=move_send.at[quarter],
            recv_sem=move_recv.at[quarter],
            device_id=(partner, tensor),
            device_id_type=MESH,
        )
        move.start()
        moves.append(move)

    query_rows = queries[...].astype(jnp.float32)
    attended = []
    for slot in range(2):
        attended.append(
            attend_row(
                query_rows[slot : slot + 1], key_rows[slot : slot + 1], value_rows[slot : slot + 1],
                keys.at[slot], values.at[slot], lengths[replica * 2 + slot],
            )
        )
    attended = jnp.concatenate(attended + [jnp.zeros((6, attended[0].shape[1]), jnp.float32)], axis=0)
    attended = attended.astype(jnp.bfloat16)

    weight_load.wait()
    for piece in range(4):
        product = jnp.dot(
            attended, weights[:, piece * 1024 : (piece + 1) * 1024], preferred_element_type=jnp.float32
        )
        partial[piece] = as_rows(product[0:2])
    residual = hidden[:, pl.ds(pl.multiple_of(tensor * 1024, 1024), 1024)].astype(jnp.float32)
    partial[tensor] = partial[tensor] + as_rows(residual)

    shares = []
    for k in range(8):
        if k == 0:
            continue
        piece = (tensor + k) % 4
        share = pltpu.make_async_remote_copy(
            src_ref=partial.at[piece],
            dst_ref=partial_in.at[k],
            send_sem=part_send.at[k],
            recv_sem=part_recv.at[k],
            device_id=((replica, partner)[k // 4], piece),
            device_id_type=MESH,
        )
        share.start()
        shares.append(share)
    for share in shares:
        share.wait()
    here = partial[tensor] + partial_in[1] + partial_in[2] + partial_in[3]
    there = partial_in[4] + partial_in[5] + partial_in[6] + partial_in[7]
    coming = jnp.where(moved[partner] == 1, there[8:16], there[0:8])
    lines = [
        as_line(jnp.where(leaving == slot, coming, here[slot * 8 : slot * 8 + 8])) for slot in range(2)
    ]
    layer_out[...] = jnp.concatenate(lines, axis=0).astype(jnp.bfloat16)

    for move in moves:
        move.wait()


def place_kernel(lengths, moved, new_key, new_value, cache_keys, cache_values, arrived, keys_out, values_out):
    chunk, slot = pl.program_id(0), pl.program_id(1)
    replica = lax.axis_index("replica")
    partner = (replica + 32) % 64
    rows = cache_keys.shape[1]
    comes = moved[replica] == slot
    length = lengths[replica * 2 + slot]
    arriving_length = lengths[partner * 2 + jnp.maximum(moved[partner], 0)]
    in_tile = lax.broadcasted_iota(jnp.int32, (TILE, LANES), 0)
    for kind, (fresh, source, target) in enumerate(
        ((new_key, cache_keys, keys_out), (new_value, cache_values, values_out))
    ):
        fresh_rows = fresh[...].astype(jnp.float32)
        fresh_row = jnp.where(slot == 1, fresh_rows[1:2], fresh_rows[0:1])
        for half in range(2):
            lanes = slice(half * LANES, (half + 1) * LANES)
            line = jnp.broadcast_to(fresh_row[:, lanes], (TILE, LANES))
            for block in range(rows // TILE):
                position = in_tile + (chunk * rows + block * TILE)
                span = slice(block * TILE, (block + 1) * TILE)
                own = source[0, span, lanes].astype(jnp.float32)
                own = jnp.where(position < length, own, jnp.where(position == length, line, 0.0))
                came = arrived[(kind * 2 + half) * 4 + block % 4, block // 4].astype(jnp.float32)
                came = jnp.where(position <= arriving_length, came, 0.0)
                target[0, span, lanes] = jnp.where(comes, came, own).astype(jnp.bfloat16)


def shards(
    hidden, queries, new_key, new_value, cache_keys, cache_values, w_out, lengths, moved_slot
):
    slots, cap, width = cache_keys.shape
    depth = cap // TILE // 4
    any_spec = pl.BlockSpec(memory_space=pl.ANY)
    vmem_spec = pl.BlockSpec(memory_space=pltpu.VMEM)
    smem_spec = pl.BlockSpec(memory_space=pltpu.SMEM)

    layer_out, arrived = pl.pallas_call(
        functools.partial(move_kernel, depth),
        out_shape=(
            jax.ShapeDtypeStruct((slots, w_out.shape[1] // 4), jnp.bfloat16),
            jax.ShapeDtypeStruct((16, cap // TILE // 4, TILE, LANES), jnp.bfloat16),
        ),
        in_specs=[smem_spec] * 2 + [vmem_spec] * 4 + [any_spec] * 3,
        out_specs=(vmem_spec, any_spec),
        scratch_shapes=[
            pltpu.VMEM((slots, cap, width), jnp.bfloat16),
            pltpu.VMEM((slots, cap, width), jnp.bfloat16),
            pltpu.VMEM(w_out.shape, jnp.bfloat16),
            pltpu.VMEM((16, cap // TILE // 4, TILE, LANES), jnp.bfloat16),
            pltpu.VMEM((4, 16, 128), jnp.float32),
            pltpu.VMEM((8, 16, 128), jnp.float32),
            pltpu.SemaphoreType.DMA((2,)),
            pltpu.SemaphoreType.DMA,
            pltpu.SemaphoreType.DMA((4,)),
            pltpu.SemaphoreType.DMA((4,)),
            pltpu.SemaphoreType.DMA((8,)),
            pltpu.SemaphoreType.DMA((8,)),
        ],
        compiler_params=pltpu.CompilerParams(
            collective_id=0, has_side_effects=True, vmem_limit_bytes=56 * 2**20
        ),
        name="move",
    )(lengths, moved_slot, hidden, queries, new_key, new_value, cache_keys, cache_values, w_out)

    chunks = 3
    cache_spec = pl.BlockSpec((1, cap // chunks, width), lambda c, s: (s, c, 0))
    keys_out, values_out = pl.pallas_call(
        place_kernel,
        grid=(chunks, slots),
        out_shape=(jax.ShapeDtypeStruct(cache_keys.shape, cache_keys.dtype),) * 2,
        in_specs=[
            smem_spec, smem_spec, vmem_spec, vmem_spec, cache_spec, cache_spec,
            pl.BlockSpec((16, cap // TILE // 4 // chunks, TILE, LANES), lambda c, s: (0, c, 0, 0)),
        ],
        out_specs=(cache_spec, cache_spec),
        compiler_params=pltpu.CompilerParams(vmem_limit_bytes=56 * 2**20),
        name="place",
    )(lengths, moved_slot, new_key, new_value, cache_keys, cache_values, arrived)
    return layer_out, keys_out, values_out


def solution(mesh):
    return jax.shard_map(
        shards,
        mesh=mesh,
        in_specs=(
            P("replica", None),
            P("replica", "tensor"),
            P("replica", "tensor"),
            P("replica", "tensor"),
            P("replica", None, "tensor"),
            P("replica", None, "tensor"),
            P("tensor", None),
            P(),
            P(),
        ),
        out_specs=(
            P("replica", "tensor"),
            P("replica", None, "tensor"),
            P("replica", None, "tensor"),
        ),
        check_vma=False,
    )
```

```python
import functools

import jax
import jax.numpy as jnp
from jax import lax
from jax.experimental import pallas as pl
from jax.experimental.pallas import tpu as pltpu
from jax.sharding import PartitionSpec as P

HEAD_DIM = 128
TILE = 16
LANES = 256
MESH = pl.DeviceIdType.MESH

OFFSETS = ((0, 0), (1, 0), (3, 0), (0, 1), (0, 3), (1, 1), (3, 3), (1, 3), (3, 1), (2, 0), (0, 2))
K = len(OFFSETS)
SHORT = 36
CHUNKS = ((0, 4), (4, 8), (8, -(-SHORT * 4 // K)))
LEVELS = ((31, 25, 21), (39, 32, 29))
DIRECT_SHORT = ((0, 4), (4, 8), (8, -(-SHORT * 4 // K)))
DIRECT_WHOLE = ((0, 4), (4, 8), (8, 12), (12, 18))


def block_diagonal(row, heads):
    width = row.shape[1]
    row_id = lax.broadcasted_iota(jnp.int32, (8, width), 0)
    col_id = lax.broadcasted_iota(jnp.int32, (8, width), 1)
    own = (col_id >= row_id * HEAD_DIM) & (col_id < row_id * HEAD_DIM + HEAD_DIM)
    return own, jnp.where(own, jnp.broadcast_to(row, (8, width)), 0.0)


def attend_row(query, fresh_key, fresh_value, keys_ref, values_ref, length):
    width = keys_ref.shape[1]
    own, query_block = block_diagonal(query, width // HEAD_DIM)
    scale = HEAD_DIM**-0.5
    scores = lax.dot_general(
        query_block.astype(jnp.bfloat16), keys_ref[...], (((1,), (1,)), ((), ())), preferred_element_type=jnp.float32
    )
    scores = scores * scale
    fresh_score = jnp.sum(query_block * fresh_key, axis=1, keepdims=True) * scale
    position = lax.broadcasted_iota(jnp.int32, scores.shape, 1)
    live = position < length
    peak = jnp.maximum(jnp.max(jnp.where(live, scores, -1e30), axis=1, keepdims=True), fresh_score)
    terms = jnp.where(live, jnp.exp(jnp.minimum(scores - peak, 0.0)), 0.0)
    fresh_term = jnp.exp(fresh_score - peak)
    total = jnp.sum(terms, axis=1, keepdims=True) + fresh_term
    weights = (terms / total).astype(jnp.bfloat16)
    fresh_weight = (fresh_term / total).astype(jnp.bfloat16).astype(jnp.float32)
    mixed = lax.dot_general(
        weights, values_ref[...], (((1,), (0,)), ((), ())), preferred_element_type=jnp.float32
    )
    mixed = mixed + fresh_weight * fresh_value
    return jnp.sum(jnp.where(own, mixed, 0.0), axis=0, keepdims=True)


def as_rows(two_rows):
    count = two_rows.shape[1] // 128
    pieces = [two_rows[s : s + 1, j * 128 : (j + 1) * 128] for s in range(2) for j in range(count)]
    return jnp.concatenate(pieces, axis=0)


def as_line(rows):
    return jnp.concatenate([rows[j : j + 1, :] for j in range(rows.shape[0])], axis=1)


def replica_at(plane, x, y):
    return plane * 16 + (x % 4) * 4 + y % 4


def block_range(chunk, blocks):
    return chunk[0] * K // 4, min(blocks, chunk[1] * K // 4)


def move_kernel(
    chunks, slots, blocks,
    lengths, moved, hidden, queries, new_key, new_value, cache_keys, cache_values, w_out,
    small_out, arrived,
    keys, values, weights, partial, partial_in, fresh_out, fresh_in, landed,
    load_sem, part_send, part_recv, along_send, along_recv, out_send, out_recv, back_send, back_recv, store_sem,
    *buffers,
):
    spread = slots is not None
    count = len(chunks)
    outgoing, buffers = buffers[:count], buffers[count:]
    final, buffers = buffers[:count], buffers[count:]
    if spread:
        held, buffers = buffers[:count], buffers[count:]
        packed, buffers = buffers[:count], buffers[count:]
        unpacked, buffers = buffers[:count], buffers[count:]
        back = buffers
    replica = lax.axis_index("replica")
    tensor = lax.axis_index("tensor")
    plane, x, y = replica // 16, (replica // 4) % 4, replica % 4
    partner = (replica + 32) % 64

    loads = []
    for i, (source, target) in enumerate(((cache_keys, keys), (cache_values, values), (w_out, weights))):
        load = pltpu.make_async_copy(source, target, load_sem.at[i])
        load.start()
        loads.append(load)

    peers = [(replica, (tensor + k) % 4) for k in range(1, 4)]
    peers += [(partner, (tensor + k) % 4) for k in range(4)]
    if spread:
        peers += [(replica_at(plane, x + dx, y + dy), tensor) for dx, dy in OFFSETS[1:]]
    barrier = pltpu.get_barrier_semaphore()
    for peer in peers:
        pl.semaphore_signal(barrier, inc=1, device_id=peer, device_id_type=MESH)

    leaving = moved[replica]
    leaving_slot = jnp.maximum(leaving, 0)

    def items_of(source):
        slot = moved[source]
        length = lengths[source * 2 + jnp.maximum(slot, 0)]
        units = lax.div(length + TILE, TILE) * 4
        return jnp.where(slot >= 0, lax.div(units + (K - 1), K), 0)

    def send(source, target, device, send_sem, recv_sem):
        copy = pltpu.make_async_remote_copy(
            src_ref=source, dst_ref=target, send_sem=send_sem, recv_sem=recv_sem,
            device_id=device, device_id_type=MESH,
        )
        copy.start()
        return copy

    def copy_units(chunk, body):
        low, high = block_range(chunk, blocks)

        def step(block, carry):
            for quarter in range(4):
                unit = block * 4 + quarter
                body(block, quarter, unit % K, unit // K - chunk[0])
            return carry

        lax.fori_loop(low, high, step, 0)

    loads[0].wait()
    loads[1].wait()
    sent_out, sent_along, sent_back = [], [], []
    for c, chunk in enumerate(chunks):
        def pack(block, quarter, relay, item, c=c):
            held_rows = (keys, values)[quarter // 2]
            lanes = slice(quarter % 2 * LANES, (quarter % 2 + 1) * LANES)
            outgoing[c][relay, item] = held_rows[leaving_slot, pl.ds(block * TILE, TILE), lanes]

        copy_units(chunk, pack)
        if c == 0:
            pl.semaphore_wait(barrier, len(peers))
        if spread:
            sent = []
            for k in range(1, K):
                dx, dy = OFFSETS[k]
                sent.append(
                    send(
                        outgoing[c].at[k], held[c].at[k], (replica_at(plane, x + dx, y + dy), tensor),
                        out_send.at[c * K + k], out_recv.at[c * K + k],
                    )
                )
            sent_out.append(sent)

            def keep(item, carry, c=c):
                held[c][0, item] = outgoing[c][0, item]
                return carry

            lax.fori_loop(0, chunk[1] - chunk[0], keep, 0)
        else:
            sent_along.append(send(outgoing[c], final[c], (partner, tensor), along_send.at[c], along_recv.at[c]))

    def along(c):
        for copy in sent_out[c]:
            copy.wait_recv()
        low, high = chunks[c]
        counts, ends, total = [], [], 0
        for dx, dy in OFFSETS:
            live = jnp.clip(items_of(replica_at(plane, x - dx, y - dy)) - low, 0, high - low)
            total = total + live
            counts.append(live)
            ends.append(total)

        def step(slot, carry):
            source, base = 0, 0
            for live, end in zip(counts[:-1], ends[:-1]):
                past = slot >= end
                source = source + jnp.where(past, 1, 0)
                base = base + jnp.where(past, live, 0)
            packed[c][slot] = held[c][source, jnp.minimum(slot - base, high - low - 1)]
            return carry

        lax.fori_loop(0, slots[c], step, 0)
        sent_along.append(send(packed[c], unpacked[c], (partner, tensor), along_send.at[c], along_recv.at[c]))

    def spread_back(c):
        sent_along[c].wait_recv()
        low, high = chunks[c]
        starts, total = [], 0
        for dx, dy in OFFSETS:
            live = jnp.clip(items_of(replica_at((plane + 2) % 4, x - dx, y - dy)) - low, 0, high - low)
            starts.append(total)
            total = total + live

        def step(item, carry):
            for k in range(K):
                slot = jnp.minimum(starts[k] + item, slots[c] - 1)
                target = final if k == 0 else back
                target[c][k, item] = unpacked[c][slot]
            return carry

        lax.fori_loop(0, high - low, step, 0)
        sent = []
        for k in range(1, K):
            dx, dy = OFFSETS[k]
            sent.append(
                send(
                    back[c].at[k], final[c].at[k], (replica_at(plane, x - dx, y - dy), tensor),
                    back_send.at[c * K + k], back_recv.at[c * K + k],
                )
            )
        sent_back.append(sent)

    query_rows = queries[...].astype(jnp.float32)
    key_rows = new_key[...].astype(jnp.float32)
    value_rows = new_value[...].astype(jnp.float32)
    fresh_out[0:8] = as_rows(key_rows)
    fresh_out[8:16] = as_rows(value_rows)
    attended = []
    for slot in range(2):
        attended.append(
            attend_row(
                query_rows[slot : slot + 1], key_rows[slot : slot + 1], value_rows[slot : slot + 1],
                keys.at[slot], values.at[slot], lengths[replica * 2 + slot],
            )
        )
    attended = jnp.concatenate(attended + [jnp.zeros((6, attended[0].shape[1]), jnp.float32)], axis=0)
    attended = attended.astype(jnp.bfloat16)

    if spread:
        along(0)

    loads[2].wait()
    for piece in range(4):
        product = jnp.dot(
            attended, weights[:, piece * 1024 : (piece + 1) * 1024], preferred_element_type=jnp.float32
        )
        partial[piece] = as_rows(product[0:2])
    residual = hidden[:, pl.ds(pl.multiple_of(tensor * 1024, 1024), 1024)].astype(jnp.float32)
    partial[tensor] = partial[tensor] + as_rows(residual)

    shares = [send(fresh_out, fresh_in, (partner, tensor), part_send.at[0], part_recv.at[0])]
    for k in range(1, 8):
        piece = (tensor + k) % 4
        shares.append(
            send(
                partial.at[piece], partial_in.at[k], ((replica, partner)[k // 4], piece),
                part_send.at[k], part_recv.at[k],
            )
        )

    if spread:
        along(1)
        spread_back(0)
        along(2)

    for share in shares:
        share.wait()
    here = partial[tensor] + partial_in[1] + partial_in[2] + partial_in[3]
    there = partial_in[4] + partial_in[5] + partial_in[6] + partial_in[7]
    coming = jnp.where(moved[partner] == 1, there[8:16], there[0:8])
    for slot in range(2):
        small_out[slot * 8 : slot * 8 + 8] = jnp.where(leaving == slot, coming, here[slot * 8 : slot * 8 + 8])
    small_out[16:32] = fresh_in[...]

    if spread:
        spread_back(1)

    stores = []
    for c, chunk in enumerate(chunks):
        if spread:
            if c == count - 1:
                spread_back(c)
            for copy in sent_back[c]:
                copy.wait_recv()
        else:
            sent_along[c].wait_recv()

        def unpack(block, quarter, relay, item, c=c):
            lanes = slice(quarter % 2 * LANES, (quarter % 2 + 1) * LANES)
            landed[quarter // 2, pl.ds(block * TILE, TILE), lanes] = final[c][relay, item]

        copy_units(chunk, unpack)
        low, high = block_range(chunk, blocks)
        for kind in range(2):
            span = slice(low * TILE, high * TILE)
            store = pltpu.make_async_copy(
                landed.at[kind, span], arrived.at[kind, span], store_sem.at[c * 2 + kind]
            )
            store.start()
            stores.append(store)
    for sent in sent_out + [sent_along] + sent_back:
        for copy in sent:
            copy.wait_send()
    for store in stores:
        store.wait()


def move(chunks, slots, blocks, collective_id, *operands):
    cache_keys, w_out = operands[6], operands[8]
    here, cap, width = cache_keys.shape
    count = len(chunks)
    any_spec = pl.BlockSpec(memory_space=pl.ANY)
    vmem_spec = pl.BlockSpec(memory_space=pltpu.VMEM)
    smem_spec = pl.BlockSpec(memory_space=pltpu.SMEM)

    def items(kind=1):
        return [pltpu.VMEM((K, high - low, TILE, LANES), jnp.bfloat16) for low, high in chunks]

    buffers = items() + items()
    if slots is not None:
        on_the_way = [pltpu.VMEM((size, TILE, LANES), jnp.bfloat16) for size in slots]
        buffers += items() + on_the_way + on_the_way + items()
    return pl.pallas_call(
        functools.partial(move_kernel, chunks, slots, blocks),
        out_shape=(
            jax.ShapeDtypeStruct((32, 128), jnp.float32),
            jax.ShapeDtypeStruct((2, cap, width), jnp.bfloat16),
        ),
        in_specs=[smem_spec] * 2 + [vmem_spec] * 4 + [any_spec] * 3,
        out_specs=(vmem_spec, any_spec),
        scratch_shapes=[
            pltpu.VMEM((here, cap, width), jnp.bfloat16),
            pltpu.VMEM((here, cap, width), jnp.bfloat16),
            pltpu.VMEM(w_out.shape, jnp.bfloat16),
            pltpu.VMEM((4, 16, 128), jnp.float32),
            pltpu.VMEM((8, 16, 128), jnp.float32),
            pltpu.VMEM((16, 128), jnp.float32),
            pltpu.VMEM((16, 128), jnp.float32),
            pltpu.VMEM((2, cap, width), jnp.bfloat16),
            pltpu.SemaphoreType.DMA((3,)),
            pltpu.SemaphoreType.DMA((8,)),
            pltpu.SemaphoreType.DMA((8,)),
            pltpu.SemaphoreType.DMA((count,)),
            pltpu.SemaphoreType.DMA((count,)),
            pltpu.SemaphoreType.DMA((count * K,)),
            pltpu.SemaphoreType.DMA((count * K,)),
            pltpu.SemaphoreType.DMA((count * K,)),
            pltpu.SemaphoreType.DMA((count * K,)),
            pltpu.SemaphoreType.DMA((2 * count,)),
            *buffers,
        ],
        compiler_params=pltpu.CompilerParams(
            collective_id=collective_id, has_side_effects=True, vmem_limit_bytes=56 * 2**20
        ),
        name="move%d" % collective_id,
    )(*operands)


def place_kernel(
    lengths, moved, new_key, new_value, small, cache_keys, cache_values, arrived,
    layer_out, keys_out, values_out,
    rows, read_sem, write_sem,
):
    replica = lax.axis_index("replica")
    partner = (replica + 32) % 64
    arriving_length = lengths[partner * 2 + jnp.maximum(moved[partner], 0)]
    arriving_slot = moved[partner]
    sources, targets = (cache_keys, cache_values), (keys_out, values_out)
    jobs = [(slot, kind) for slot in range(2) for kind in range(2)]
    for slot, kind in jobs:
        comes = moved[replica] == slot

        @pl.when(comes)
        def _(slot=slot, kind=kind):
            pltpu.make_async_copy(arrived.at[kind], rows.at[slot, kind], read_sem.at[slot * 2 + kind]).start()

        @pl.when(jnp.logical_not(comes))
        def _(slot=slot, kind=kind):
            pltpu.make_async_copy(sources[kind].at[slot], rows.at[slot, kind], read_sem.at[slot * 2 + kind]).start()

    layer_out[...] = jnp.concatenate([as_line(small[0:8]), as_line(small[8:16])], axis=0).astype(jnp.bfloat16)
    cap, width = rows.shape[2:]
    in_tile = lax.broadcasted_iota(jnp.int32, (TILE, width), 0)
    writes = []
    for slot, kind in jobs:
        comes = moved[replica] == slot
        length = jnp.where(comes, arriving_length, lengths[replica * 2 + slot])
        own_fresh = (new_key, new_value)[kind][...].astype(jnp.float32)[slot : slot + 1]
        come_fresh = small[16 + kind * 8 : 24 + kind * 8]
        come_fresh = as_line(jnp.where(arriving_slot == 1, come_fresh[4:8], come_fresh[0:4]))
        fresh = jnp.broadcast_to(jnp.where(comes, come_fresh, own_fresh), (TILE, width))
        pltpu.make_async_copy(sources[kind].at[slot], rows.at[slot, kind], read_sem.at[slot * 2 + kind]).wait()
        last = lax.div(length, TILE)
        span = pl.ds(pl.multiple_of(last * TILE, TILE), TILE)
        position = in_tile + last * TILE
        edge = rows[slot, kind, span, :].astype(jnp.float32)
        edge = jnp.where(position < length, edge, jnp.where(position == length, fresh, 0.0))
        rows[slot, kind, span, :] = edge.astype(jnp.bfloat16)

        def clear(block, carry, slot=slot, kind=kind):
            dead = pl.ds(pl.multiple_of(block * TILE, TILE), TILE)
            rows[slot, kind, dead, :] = jnp.zeros((TILE, width), jnp.bfloat16)
            return carry

        lax.fori_loop(last + 1, cap // TILE, clear, 0)
        write = pltpu.make_async_copy(rows.at[slot, kind], targets[kind].at[slot], write_sem.at[slot * 2 + kind])
        write.start()
        writes.append(write)
    for write in writes:
        write.wait()


def choose_kernel(lengths, moved, choice):
    row = lax.broadcasted_iota(jnp.int32, (64, 64), 0)
    col = lax.broadcasted_iota(jnp.int32, (64, 64), 1)
    slot = jnp.sum(jnp.where(row == col, moved[...].astype(jnp.float32), 0.0), axis=1, keepdims=True)
    moves = slot >= 0.0
    wide_row = lax.broadcasted_iota(jnp.int32, (64, 128), 0)
    wide_col = lax.broadcasted_iota(jnp.int32, (64, 128), 1)
    wanted = wide_col.astype(jnp.float32) == 2.0 * wide_row.astype(jnp.float32) + jnp.maximum(slot, 0.0)
    length = jnp.sum(jnp.where(wanted, lengths[...].astype(jnp.float32), 0.0), axis=1, keepdims=True)
    blocks = jnp.where(moves, jnp.floor((length + TILE) * (1.0 / TILE)), 0.0)
    items = jnp.floor((blocks * 4.0 + (K - 0.5)) * (1.0 / K))
    longest = jnp.max(blocks).astype(jnp.int32)
    relays = row < 0
    for dx, dy in OFFSETS:
        there = (row & 48) + ((((row >> 2) + dx) & 3) << 2) + ((row + dy) & 3)
        relays = relays | (there == col)
    needs = []
    for low, high in CHUNKS:
        live = jnp.clip(items - low, 0.0, float(high - low))
        needs.append(jnp.max(jnp.sum(jnp.where(relays, live, 0.0), axis=0)).astype(jnp.int32))
    result = 0
    for level in LEVELS:
        fits = longest <= SHORT
        for need, size in zip(needs, level):
            fits = fits & (need <= size)
        result = result + jnp.where(fits, 0, 1)
    choice[0] = result + jnp.where(longest <= SHORT, 0, 1)


def shards(
    hidden, queries, new_key, new_value, cache_keys, cache_values, w_out, lengths, moved_slot
):
    slots, cap, width = cache_keys.shape
    any_spec = pl.BlockSpec(memory_space=pl.ANY)
    vmem_spec = pl.BlockSpec(memory_space=pltpu.VMEM)
    smem_spec = pl.BlockSpec(memory_space=pltpu.SMEM)

    choice = pl.pallas_call(
        choose_kernel,
        out_shape=jax.ShapeDtypeStruct((1,), jnp.int32),
        in_specs=[vmem_spec] * 2,
        out_specs=smem_spec,
        name="choose",
    )(lengths.reshape(1, -1), moved_slot.reshape(1, -1))

    builds = [functools.partial(move, CHUNKS, level, SHORT, i) for i, level in enumerate(LEVELS)]
    builds.append(functools.partial(move, DIRECT_SHORT, None, SHORT, len(builds)))
    builds.append(functools.partial(move, DIRECT_WHOLE, None, cap // TILE, len(builds)))
    small, arrived = lax.switch(
        choice[0], builds,
        lengths, moved_slot, hidden, queries, new_key, new_value, cache_keys, cache_values, w_out,
    )

    return pl.pallas_call(
        place_kernel,
        out_shape=(
            jax.ShapeDtypeStruct((slots, w_out.shape[1] // 4), jnp.bfloat16),
            jax.ShapeDtypeStruct(cache_keys.shape, cache_keys.dtype),
            jax.ShapeDtypeStruct(cache_keys.shape, cache_keys.dtype),
        ),
        in_specs=[smem_spec] * 2 + [vmem_spec] * 3 + [any_spec] * 3,
        out_specs=(vmem_spec, any_spec, any_spec),
        scratch_shapes=[
            pltpu.VMEM((slots, 2, cap, width), jnp.bfloat16),
            pltpu.SemaphoreType.DMA((4,)),
            pltpu.SemaphoreType.DMA((4,)),
        ],
        compiler_params=pltpu.CompilerParams(vmem_limit_bytes=56 * 2**20),
        name="place",
    )(lengths, moved_slot, new_key, new_value, small, cache_keys, cache_values, arrived)


def solution(mesh):
    return jax.shard_map(
        shards,
        mesh=mesh,
        in_specs=(
            P("replica", None),
            P("replica", "tensor"),
            P("replica", "tensor"),
            P("replica", "tensor"),
            P("replica", None, "tensor"),
            P("replica", None, "tensor"),
            P("tensor", None),
            P(),
            P(),
        ),
        out_specs=(
            P("replica", "tensor"),
            P("replica", None, "tensor"),
            P("replica", None, "tensor"),
        ),
        check_vma=False,
    )
```

```python
import functools

import jax
import jax.numpy as jnp
from jax import lax
from jax.experimental import pallas as pl
from jax.experimental.pallas import tpu as pltpu
from jax.sharding import PartitionSpec as P

HEAD_DIM = 128
TILE = 16
LANES = 256
MESH = pl.DeviceIdType.MESH

OFFSETS = tuple((dx, dy) for dx in range(4) for dy in range(4))
K = len(OFFSETS)
STEP = K // 4
SHORT = 36
CHUNKS = ((0, 1), (1, 4), (4, 6), (6, 9))
LEVELS = ((0, 21, 12, 12), (0, 26, 14, 16), (0, 31, 18, 19))
DIRECT = (0, 0, 0, 0)
WHOLE = ((0, 3), (3, 6), (6, 9), (9, 12))
PART = 128
SPLIT = 256


def block_diagonal(row, heads):
    width = row.shape[1]
    row_id = lax.broadcasted_iota(jnp.int32, (8, width), 0)
    col_id = lax.broadcasted_iota(jnp.int32, (8, width), 1)
    own = (col_id >= row_id * HEAD_DIM) & (col_id < row_id * HEAD_DIM + HEAD_DIM)
    return own, jnp.where(own, jnp.broadcast_to(row, (8, width)), 0.0)


def attend_row(query, fresh_key, fresh_value, keys_ref, values_ref, length):
    width = keys_ref.shape[1]
    own, query_block = block_diagonal(query, width // HEAD_DIM)
    scale = HEAD_DIM**-0.5
    scores = lax.dot_general(
        query_block.astype(jnp.bfloat16), keys_ref[...], (((1,), (1,)), ((), ())), preferred_element_type=jnp.float32
    )
    scores = scores * scale
    fresh_score = jnp.sum(query_block * fresh_key, axis=1, keepdims=True) * scale
    position = lax.broadcasted_iota(jnp.int32, scores.shape, 1)
    live = position < length
    peak = jnp.maximum(jnp.max(jnp.where(live, scores, -1e30), axis=1, keepdims=True), fresh_score)
    terms = jnp.where(live, jnp.exp(jnp.minimum(scores - peak, 0.0)), 0.0)
    fresh_term = jnp.exp(fresh_score - peak)
    total = jnp.sum(terms, axis=1, keepdims=True) + fresh_term
    weights = (terms / total).astype(jnp.bfloat16)
    fresh_weight = (fresh_term / total).astype(jnp.bfloat16).astype(jnp.float32)
    mixed = lax.dot_general(
        weights, values_ref[...], (((1,), (0,)), ((), ())), preferred_element_type=jnp.float32
    )
    mixed = mixed + fresh_weight * fresh_value
    return jnp.sum(jnp.where(own, mixed, 0.0), axis=0, keepdims=True)


def as_rows(two_rows):
    count = two_rows.shape[1] // 128
    pieces = [two_rows[s : s + 1, j * 128 : (j + 1) * 128] for s in range(2) for j in range(count)]
    return jnp.concatenate(pieces, axis=0)


def as_line(rows):
    return jnp.concatenate([rows[j : j + 1, :] for j in range(rows.shape[0])], axis=1)


def replica_at(plane, x, y):
    return plane * 16 + (x % 4) * 4 + y % 4


def items_in(blocks):
    return (blocks + (STEP - 1)) * (128 // STEP + 1) >> 7 if STEP == 3 else (blocks + (STEP - 1)) >> (STEP.bit_length() - 1)


def move_kernel(
    chunks, slots,
    lengths, moved, hidden, queries, new_key, new_value, cache_keys, cache_values, w_out,
    small_out, arrived,
    keys, values, weights, partial, partial_in, fresh_out, fresh_in, landed,
    load_sem, part_send, part_recv, along_send, along_recv, out_send, out_recv, back_send, back_recv, store_sem,
    *buffers,
):
    count = len(chunks)
    outgoing, buffers = buffers[:count], buffers[count:]
    final, buffers = buffers[:count], buffers[count:]
    held, packed, unpacked, back = {}, {}, {}, {}
    spread = [c for c in range(count) if slots[c]]
    for i, c in enumerate(spread):
        held[c], packed[c], unpacked[c], back[c] = buffers[i * 4 : i * 4 + 4]
    replica = lax.axis_index("replica")
    tensor = lax.axis_index("tensor")
    plane, x, y = replica // 16, (replica // 4) % 4, replica % 4
    partner = (replica + 32) % 64

    loads = []
    parts = [(cache, held_rows, span) for span in (slice(0, SPLIT), slice(SPLIT, None)) for cache, held_rows in ((cache_keys, keys), (cache_values, values))]
    for i, (cache, held_rows, span) in enumerate(parts):
        loads.append(pltpu.make_async_copy(cache.at[:, span], held_rows.at[:, span], load_sem.at[i]))
    loads.append(pltpu.make_async_copy(w_out, weights, load_sem.at[4]))
    for load in loads:
        load.start()

    peers = [(replica, (tensor + k) % 4) for k in range(1, 4)]
    peers += [(partner, (tensor + k) % 4) for k in range(4)]
    if spread:
        peers += [(replica_at(plane, x + dx, y + dy), tensor) for dx, dy in OFFSETS[1:]]
    barrier = pltpu.get_barrier_semaphore()
    for peer in peers:
        pl.semaphore_signal(barrier, inc=1, device_id=peer, device_id_type=MESH)

    leaving = moved[replica]

    def items_of(source):
        slot = moved[source]
        length = lengths[source * 2 + jnp.maximum(slot, 0)]
        return jnp.where(slot >= 0, items_in((length + TILE) >> 4), 0)

    def send(source, target, device, send_sem, recv_sem):
        copy = pltpu.make_async_remote_copy(
            src_ref=source, dst_ref=target, send_sem=send_sem, recv_sem=recv_sem,
            device_id=device, device_id_type=MESH,
        )
        copy.start()
        return copy

    def copy_units(chunk, body):
        def step(item, carry):
            for k in range(K):
                rows = pl.ds(pl.multiple_of((item * STEP + k // 4) * TILE, TILE), TILE)
                lanes = slice(k % 2 * LANES, (k % 2 + 1) * LANES)
                body(k % 4 // 2, rows, lanes, k, item - chunk[0])
            return carry

        lax.fori_loop(chunk[0], chunk[1], step, 0)

    waited = 0
    sent_out, sent_along, sent_back = {}, {}, {}
    for c, chunk in enumerate(chunks):
        if c == 0 or (waited == 2 and chunk[1] * STEP * TILE > SPLIT):
            loads[waited].wait()
            loads[waited + 1].wait()
            waited += 2
            if chunk[1] * STEP * TILE > SPLIT and waited == 2:
                loads[2].wait()
                loads[3].wait()
                waited = 4

        def pack(kind, rows, lanes, relay, item, c=c):
            held_rows = (keys, values)[kind]
            outgoing[c][relay, item] = jnp.where(leaving == 1, held_rows[1, rows, lanes], held_rows[0, rows, lanes])

        copy_units(chunk, pack)
        if c == 0:
            pl.semaphore_wait(barrier, len(peers))
        if not slots[c]:
            sent_along[c] = send(outgoing[c], final[c], (partner, tensor), along_send.at[c], along_recv.at[c])
            continue
        sent_out[c] = []
        for k in range(1, K):
            dx, dy = OFFSETS[k]
            sent_out[c].append(
                send(
                    outgoing[c].at[k], held[c].at[k], (replica_at(plane, x + dx, y + dy), tensor),
                    out_send.at[c * K + k], out_recv.at[c * K + k],
                )
            )

        def keep(item, carry, c=c):
            held[c][0, item] = outgoing[c][0, item]
            return carry

        lax.fori_loop(0, chunk[1] - chunk[0], keep, 0)
    if waited == 2:
        loads[2].wait()
        loads[3].wait()

    if spread:
        leave_items = [items_of(replica_at(plane, x - dx, y - dy)) for dx, dy in OFFSETS]
        come_items = [items_of(replica_at((plane + 2) % 4, x - dx, y - dy)) for dx, dy in OFFSETS]

    def along(c):
        for copy in sent_out[c]:
            copy.wait_recv()
        low, high = chunks[c]
        counts, ends, total = [], [], 0
        for items in leave_items:
            live = jnp.clip(items - low, 0, high - low)
            total = total + live
            counts.append(live)
            ends.append(total)

        def step(slot, carry):
            source, base = 0, 0
            for live, end in zip(counts[:-1], ends[:-1]):
                past = slot >= end
                source = source + jnp.where(past, 1, 0)
                base = base + jnp.where(past, live, 0)
            item = jnp.minimum(slot - base, high - low - 1)
            packed[c][slot] = held[c][source, item]
            return carry

        lax.fori_loop(0, slots[c], step, 0)
        sent_along[c] = send(packed[c], unpacked[c], (partner, tensor), along_send.at[c], along_recv.at[c])

    def spread_back(c):
        sent_along[c].wait_recv()
        low, high = chunks[c]
        starts, total = [], 0
        for items in come_items:
            starts.append(total)
            total = total + jnp.clip(items - low, 0, high - low)
        sent_back[c] = []
        for k in range(K - 1, -1, -1):
            target = final[c] if k == 0 else back[c]
            for item in range(high - low):
                target[k, item] = unpacked[c][jnp.minimum(starts[k] + item, slots[c] - 1)]
            if k:
                dx, dy = OFFSETS[k]
                sent_back[c].append(
                    send(
                        back[c].at[k], final[c].at[k], (replica_at(plane, x - dx, y - dy), tensor),
                        back_send.at[c * K + k], back_recv.at[c * K + k],
                    )
                )

    query_rows = queries[...].astype(jnp.float32)
    key_rows = new_key[...].astype(jnp.float32)
    value_rows = new_value[...].astype(jnp.float32)
    fresh_out[0:8] = as_rows(key_rows)
    fresh_out[8:16] = as_rows(value_rows)
    attended = []
    for slot in range(2):
        attended.append(
            attend_row(
                query_rows[slot : slot + 1], key_rows[slot : slot + 1], value_rows[slot : slot + 1],
                keys.at[slot], values.at[slot], lengths[replica * 2 + slot],
            )
        )
    attended = jnp.concatenate(attended + [jnp.zeros((6, attended[0].shape[1]), jnp.float32)], axis=0)
    attended = attended.astype(jnp.bfloat16)

    loads[4].wait()
    for piece in range(4):
        product = jnp.dot(
            attended, weights[:, piece * 1024 : (piece + 1) * 1024], preferred_element_type=jnp.float32
        )
        partial[piece] = as_rows(product[0:2])
    residual = hidden[:, pl.ds(pl.multiple_of(tensor * 1024, 1024), 1024)].astype(jnp.float32)
    partial[tensor] = partial[tensor] + as_rows(residual)

    shares = [send(fresh_out, fresh_in, (partner, tensor), part_send.at[0], part_recv.at[0])]
    for k in range(1, 8):
        piece = (tensor + k) % 4
        shares.append(
            send(
                partial.at[piece], partial_in.at[k], ((replica, partner)[k // 4], piece),
                part_send.at[k], part_recv.at[k],
            )
        )

    for c in spread:
        along(c)
        spread_back(c)

    for share in shares:
        share.wait()
    here = partial[tensor] + partial_in[1] + partial_in[2] + partial_in[3]
    there = partial_in[4] + partial_in[5] + partial_in[6] + partial_in[7]
    coming = jnp.where(moved[partner] == 1, there[8:16], there[0:8])
    for slot in range(2):
        small_out[slot * 8 : slot * 8 + 8] = jnp.where(leaving == slot, coming, here[slot * 8 : slot * 8 + 8])
    small_out[16:32] = fresh_in[...]

    stores = []
    for c, chunk in enumerate(chunks):
        if not slots[c]:
            sent_along[c].wait_recv()
        else:
            for copy in sent_back[c]:
                copy.wait_recv()

        def unpack(kind, rows, lanes, relay, item, c=c):
            landed[kind, rows, lanes] = final[c][relay, item]

        copy_units(chunk, unpack)
        for kind in range(2):
            span = slice(chunk[0] * STEP * TILE, chunk[1] * STEP * TILE)
            store = pltpu.make_async_copy(
                landed.at[kind, span], arrived.at[kind, span], store_sem.at[c * 2 + kind]
            )
            store.start()
            stores.append(store)
    for copy in sent_along.values():
        copy.wait_send()
    for sent in (sent_out, sent_back):
        for copies in sent.values():
            for copy in copies:
                copy.wait_send()
    for store in stores:
        store.wait()


def move(chunks, slots, collective_id, *operands):
    cache_keys, w_out = operands[6], operands[8]
    here, cap, width = cache_keys.shape
    count = len(chunks)
    any_spec = pl.BlockSpec(memory_space=pl.ANY)
    vmem_spec = pl.BlockSpec(memory_space=pltpu.VMEM)
    smem_spec = pl.BlockSpec(memory_space=pltpu.SMEM)

    def items(chunk):
        return pltpu.VMEM((K, chunk[1] - chunk[0], TILE, LANES), jnp.bfloat16)

    buffers = [items(chunk) for chunk in chunks] * 2
    for chunk, size in zip(chunks, slots):
        if size:
            on_the_way = pltpu.VMEM((size, TILE, LANES), jnp.bfloat16)
            buffers += [items(chunk), on_the_way, on_the_way, items(chunk)]
    return pl.pallas_call(
        functools.partial(move_kernel, chunks, slots),
        out_shape=(
            jax.ShapeDtypeStruct((32, 128), jnp.float32),
            jax.ShapeDtypeStruct((2, cap, width), jnp.bfloat16),
        ),
        in_specs=[smem_spec] * 2 + [vmem_spec] * 4 + [any_spec] * 3,
        out_specs=(vmem_spec, any_spec),
        scratch_shapes=[
            pltpu.VMEM((here, cap, width), jnp.bfloat16),
            pltpu.VMEM((here, cap, width), jnp.bfloat16),
            pltpu.VMEM(w_out.shape, jnp.bfloat16),
            pltpu.VMEM((4, 16, 128), jnp.float32),
            pltpu.VMEM((8, 16, 128), jnp.float32),
            pltpu.VMEM((16, 128), jnp.float32),
            pltpu.VMEM((16, 128), jnp.float32),
            pltpu.VMEM((2, cap, width), jnp.bfloat16),
            pltpu.SemaphoreType.DMA((5,)),
            pltpu.SemaphoreType.DMA((8,)),
            pltpu.SemaphoreType.DMA((8,)),
            pltpu.SemaphoreType.DMA((count,)),
            pltpu.SemaphoreType.DMA((count,)),
            pltpu.SemaphoreType.DMA((count * K,)),
            pltpu.SemaphoreType.DMA((count * K,)),
            pltpu.SemaphoreType.DMA((count * K,)),
            pltpu.SemaphoreType.DMA((count * K,)),
            pltpu.SemaphoreType.DMA((2 * count,)),
            *buffers,
        ],
        compiler_params=pltpu.CompilerParams(
            collective_id=collective_id, has_side_effects=True, vmem_limit_bytes=56 * 2**20
        ),
        name="move%d" % collective_id,
    )(*operands)


def place_kernel(
    lengths, moved, new_key, new_value, small, cache_keys, cache_values, arrived,
    layer_out, keys_out, values_out,
    zeros, rows, read_sem, write_sem,
):
    replica = lax.axis_index("replica")
    partner = (replica + 32) % 64
    arriving_length = lengths[partner * 2 + jnp.maximum(moved[partner], 0)]
    arriving_slot = moved[partner]
    cap, width = keys_out.shape[1:]
    spans = cap // PART
    jobs = []
    for slot in range(2):
        comes = moved[replica] == slot
        length = jnp.where(comes, arriving_length, lengths[replica * 2 + slot])
        last = lax.shift_right_logical(length, PART.bit_length() - 1)
        for kind, (cache, target) in enumerate(((cache_keys, keys_out), (cache_values, values_out))):
            for part in range(spans):
                span = slice(part * PART, (part + 1) * PART)
                sem = read_sem.at[(slot * 2 + kind) * spans + part]

                @pl.when((part <= last) & comes)
                def _(slot=slot, kind=kind, span=span, sem=sem):
                    pltpu.make_async_copy(arrived.at[kind, span], rows.at[slot, kind, span], sem).start()

                @pl.when((part <= last) & jnp.logical_not(comes))
                def _(slot=slot, kind=kind, span=span, sem=sem, cache=cache):
                    pltpu.make_async_copy(cache.at[slot, span], rows.at[slot, kind, span], sem).start()

            jobs.append((slot, kind, comes, length, last, cache.at[slot], target.at[slot]))
    zeros[...] = jnp.zeros_like(zeros)
    for slot, kind, comes, length, last, cache, target in jobs:
        for part in range(spans):
            span = slice(part * PART, (part + 1) * PART)

            @pl.when(part > last)
            def _(slot=slot, kind=kind, target=target, span=span, part=part):
                sem = write_sem.at[(slot * 2 + kind) * spans + part]
                pltpu.make_async_copy(zeros, target.at[span], sem).start()

    layer_out[...] = jnp.concatenate([as_line(small[0:8]), as_line(small[8:16])], axis=0).astype(jnp.bfloat16)
    in_part = lax.broadcasted_iota(jnp.int32, (PART, width), 0)
    for slot, kind, comes, length, last, cache, target in jobs:
        own_fresh = (new_key, new_value)[kind][...].astype(jnp.float32)[slot : slot + 1]
        come_fresh = small[16 + kind * 8 : 24 + kind * 8]
        come_fresh = as_line(jnp.where(arriving_slot == 1, come_fresh[4:8], come_fresh[0:4]))
        fresh = jnp.broadcast_to(jnp.where(comes, come_fresh, own_fresh), (PART, width))
        for part in range(spans):
            span = slice(part * PART, (part + 1) * PART)

            @pl.when(part <= last)
            def _(slot=slot, kind=kind, cache=cache, target=target, span=span, part=part):
                index = (slot * 2 + kind) * spans + part
                pltpu.make_async_copy(cache.at[span], rows.at[slot, kind, span], read_sem.at[index]).wait()

                @pl.when(part == last)
                def _():
                    position = in_part + part * PART
                    edge = rows[slot, kind, span].astype(jnp.float32)
                    edge = jnp.where(position < length, edge, jnp.where(position == length, fresh, 0.0))
                    rows[slot, kind, span] = edge.astype(jnp.bfloat16)

                pltpu.make_async_copy(rows.at[slot, kind, span], target.at[span], write_sem.at[index]).start()
    for slot, kind, comes, length, last, cache, target in jobs:
        for part in range(spans):
            span = slice(part * PART, (part + 1) * PART)
            sem = write_sem.at[(slot * 2 + kind) * spans + part]
            pltpu.make_async_copy(zeros, target.at[span], sem).wait()


def choose_kernel(lengths, moved, choice):
    row = lax.broadcasted_iota(jnp.int32, (64, 64), 0)
    col = lax.broadcasted_iota(jnp.int32, (64, 64), 1)
    slot = jnp.sum(jnp.where(row == col, moved[...].astype(jnp.float32), 0.0), axis=1, keepdims=True)
    moves = slot >= 0.0
    wide_row = lax.broadcasted_iota(jnp.int32, (64, 128), 0)
    wide_col = lax.broadcasted_iota(jnp.int32, (64, 128), 1)
    wanted = wide_col.astype(jnp.float32) == 2.0 * wide_row.astype(jnp.float32) + jnp.maximum(slot, 0.0)
    length = jnp.sum(jnp.where(wanted, lengths[...].astype(jnp.float32), 0.0), axis=1, keepdims=True)
    blocks = jnp.where(moves, jnp.floor((length + TILE) * (1.0 / TILE)), 0.0)
    items = jnp.floor((blocks + (STEP - 0.5)) * (1.0 / STEP))
    longest = jnp.max(blocks).astype(jnp.int32)
    relays = row < 0
    for dx, dy in OFFSETS:
        there = (row & 48) + ((((row >> 2) + dx) & 3) << 2) + ((row + dy) & 3)
        relays = relays | (there == col)
    needs = []
    for low, high in CHUNKS[1:]:
        live = jnp.clip(items - low, 0.0, float(high - low))
        needs.append(jnp.max(jnp.sum(jnp.where(relays, live, 0.0), axis=0)).astype(jnp.int32))
    result = 0
    for level in LEVELS:
        fits = longest <= SHORT
        for need, size in zip(needs, level[1:]):
            fits = fits & (need <= size)
        result = result + jnp.where(fits, 0, 1)
    choice[0] = result + jnp.where(longest <= SHORT, 0, 1)


def shards(
    hidden, queries, new_key, new_value, cache_keys, cache_values, w_out, lengths, moved_slot
):
    slots, cap, width = cache_keys.shape
    any_spec = pl.BlockSpec(memory_space=pl.ANY)
    vmem_spec = pl.BlockSpec(memory_space=pltpu.VMEM)
    smem_spec = pl.BlockSpec(memory_space=pltpu.SMEM)

    choice = pl.pallas_call(
        choose_kernel,
        out_shape=jax.ShapeDtypeStruct((1,), jnp.int32),
        in_specs=[vmem_spec] * 2,
        out_specs=smem_spec,
        name="choose",
    )(lengths.reshape(1, -1), moved_slot.reshape(1, -1))

    builds = [functools.partial(move, CHUNKS, level, i) for i, level in enumerate(LEVELS)]
    builds.append(functools.partial(move, CHUNKS, DIRECT, len(builds)))
    builds.append(functools.partial(move, WHOLE, DIRECT, len(builds)))
    small, arrived = lax.switch(
        choice[0], builds,
        lengths, moved_slot, hidden, queries, new_key, new_value, cache_keys, cache_values, w_out,
    )

    return pl.pallas_call(
        place_kernel,
        out_shape=(
            jax.ShapeDtypeStruct((slots, w_out.shape[1] // 4), jnp.bfloat16),
            jax.ShapeDtypeStruct(cache_keys.shape, cache_keys.dtype),
            jax.ShapeDtypeStruct(cache_keys.shape, cache_keys.dtype),
        ),
        in_specs=[smem_spec] * 2 + [vmem_spec] * 3 + [any_spec] * 3,
        out_specs=(vmem_spec, any_spec, any_spec),
        scratch_shapes=[
            pltpu.VMEM((PART, width), jnp.bfloat16),
            pltpu.VMEM((slots, 2, cap, width), jnp.bfloat16),
            pltpu.SemaphoreType.DMA((4 * cap // PART,)),
            pltpu.SemaphoreType.DMA((4 * cap // PART,)),
        ],
        compiler_params=pltpu.CompilerParams(vmem_limit_bytes=56 * 2**20),
        name="place",
    )(lengths, moved_slot, new_key, new_value, small, cache_keys, cache_values, arrived)


def solution(mesh):
    return jax.shard_map(
        shards,
        mesh=mesh,
        in_specs=(
            P("replica", None),
            P("replica", "tensor"),
            P("replica", "tensor"),
            P("replica", "tensor"),
            P("replica", None, "tensor"),
            P("replica", None, "tensor"),
            P("tensor", None),
            P(),
            P(),
        ),
        out_specs=(
            P("replica", "tensor"),
            P("replica", None, "tensor"),
            P("replica", None, "tensor"),
        ),
        check_vma=False,
    )
```

```python
import functools

import jax
import jax.numpy as jnp
from jax import lax
from jax.experimental import pallas as pl
from jax.experimental.pallas import tpu as pltpu
from jax.sharding import PartitionSpec as P

HEAD_DIM = 128
TILE = 16
LANES = 256
MESH = pl.DeviceIdType.MESH

OFFSETS = tuple((dx, dy) for dx in range(4) for dy in range(4))
K = len(OFFSETS)
STEP = K // 4
SHORT = 36
CHUNKS = ((0, 1), (1, 4), (4, 6), (6, 9))
LEVELS = ((0, 20, 10, 10), (0, 23, 12, 12), (0, 26, 14, 15), (0, 34, 18, 18))
DIRECT = (0, 0, 0, 0)
WHOLE = ((0, 3), (3, 6), (6, 9), (9, 12))
ORDER = (
    ("attend",), ("along", 1), ("settle",), ("back", 1), ("along", 2), ("finish",), ("land", 0),
    ("back", 2), ("along", 3), ("land", 1), ("back", 3), ("land", 2), ("land", 3),
)
PLAIN = (("attend",), ("settle",), ("finish",), ("land", 0), ("land", 1), ("land", 2), ("land", 3))
SPLIT = 256


def block_diagonal(row, heads):
    width = row.shape[1]
    row_id = lax.broadcasted_iota(jnp.int32, (8, width), 0)
    col_id = lax.broadcasted_iota(jnp.int32, (8, width), 1)
    own = (col_id >= row_id * HEAD_DIM) & (col_id < row_id * HEAD_DIM + HEAD_DIM)
    return own, jnp.where(own, jnp.broadcast_to(row, (8, width)), 0.0)


def attend_row(query, fresh_key, fresh_value, keys_ref, values_ref, length):
    width = keys_ref.shape[1]
    own, query_block = block_diagonal(query, width // HEAD_DIM)
    scale = HEAD_DIM**-0.5
    scores = lax.dot_general(
        query_block.astype(jnp.bfloat16), keys_ref[...], (((1,), (1,)), ((), ())), preferred_element_type=jnp.float32
    )
    scores = scores * scale
    fresh_score = jnp.sum(query_block * fresh_key, axis=1, keepdims=True) * scale
    position = lax.broadcasted_iota(jnp.int32, scores.shape, 1)
    live = position < length
    peak = jnp.maximum(jnp.max(jnp.where(live, scores, -1e30), axis=1, keepdims=True), fresh_score)
    terms = jnp.where(live, jnp.exp(jnp.minimum(scores - peak, 0.0)), 0.0)
    fresh_term = jnp.exp(fresh_score - peak)
    total = jnp.sum(terms, axis=1, keepdims=True) + fresh_term
    weights = (terms / total).astype(jnp.bfloat16)
    fresh_weight = (fresh_term / total).astype(jnp.bfloat16).astype(jnp.float32)
    mixed = lax.dot_general(
        weights, values_ref[...], (((1,), (0,)), ((), ())), preferred_element_type=jnp.float32
    )
    mixed = mixed + fresh_weight * fresh_value
    return jnp.sum(jnp.where(own, mixed, 0.0), axis=0, keepdims=True)


def as_rows(two_rows):
    count = two_rows.shape[1] // 128
    pieces = [two_rows[s : s + 1, j * 128 : (j + 1) * 128] for s in range(2) for j in range(count)]
    return jnp.concatenate(pieces, axis=0)


def as_line(rows):
    return jnp.concatenate([rows[j : j + 1, :] for j in range(rows.shape[0])], axis=1)


def replica_at(plane, x, y):
    return plane * 16 + (x % 4) * 4 + y % 4


def move_kernel(
    chunks, slots,
    lengths, moved, hidden, queries, new_key, new_value, cache_keys, cache_values, w_out,
    small_out, settled,
    keys, values, weights, partial, partial_in, fresh_out, fresh_in,
    load_sem, part_send, part_recv, along_send, along_recv, out_send, out_recv, back_send, back_recv, store_sem,
    *buffers,
):
    count = len(chunks)
    outgoing, buffers = buffers[:count], buffers[count:]
    final, buffers = buffers[:count], buffers[count:]
    held, packed, unpacked, back = {}, {}, {}, {}
    spread = [c for c in range(count) if slots[c]]
    for i, c in enumerate(spread):
        held[c], packed[c], unpacked[c], back[c] = buffers[i * 4 : i * 4 + 4]
    replica = lax.axis_index("replica")
    tensor = lax.axis_index("tensor")
    plane, x, y = replica // 16, (replica // 4) % 4, replica % 4
    partner = (replica + 32) % 64

    loads = []
    parts = [(cache, held_rows, span) for span in (slice(0, SPLIT), slice(SPLIT, None)) for cache, held_rows in ((cache_keys, keys), (cache_values, values))]
    for i, (cache, held_rows, span) in enumerate(parts):
        loads.append(pltpu.make_async_copy(cache.at[:, span], held_rows.at[:, span], load_sem.at[i]))
    loads.append(pltpu.make_async_copy(w_out, weights, load_sem.at[4]))
    for load in loads:
        load.start()

    peers = [(replica, (tensor + k) % 4) for k in range(1, 4)]
    peers += [(partner, (tensor + k) % 4) for k in range(4)]
    if spread:
        peers += [(replica_at(plane, x + dx, y + dy), tensor) for dx, dy in OFFSETS[1:]]
    barrier = pltpu.get_barrier_semaphore()
    for peer in peers:
        pl.semaphore_signal(barrier, inc=1, device_id=peer, device_id_type=MESH)

    leaving = moved[replica]

    def items_of(source, k):
        slot = moved[source]
        length = lengths[source * 2 + jnp.maximum(slot, 0)]
        return jnp.where(slot >= 0, ((length + TILE) >> 4) + (STEP - 1 - k // 4) >> (STEP.bit_length() - 1), 0)

    def send(source, target, device, send_sem, recv_sem):
        copy = pltpu.make_async_remote_copy(
            src_ref=source, dst_ref=target, send_sem=send_sem, recv_sem=recv_sem,
            device_id=device, device_id_type=MESH,
        )
        copy.start()
        return copy

    def landing(buffer, sem):
        return pltpu.make_async_remote_copy(
            src_ref=buffer, dst_ref=buffer, send_sem=sem, recv_sem=sem, device_id=(partner, tensor), device_id_type=MESH
        )

    def copy_units(chunk, body):
        def step(item, carry):
            for k in range(K):
                rows = pl.ds(pl.multiple_of((item * STEP + k // 4) * TILE, TILE), TILE)
                lanes = slice(k % 2 * LANES, (k % 2 + 1) * LANES)
                body(k % 4 // 2, rows, lanes, k, item - chunk[0])
            return carry

        lax.fori_loop(chunk[0], chunk[1], step, 0)

    waited = 0
    sent_along = {}
    for c, chunk in enumerate(chunks):
        if c == 0 or (waited == 2 and chunk[1] * STEP * TILE > SPLIT):
            loads[waited].wait()
            loads[waited + 1].wait()
            waited += 2
            if chunk[1] * STEP * TILE > SPLIT and waited == 2:
                loads[2].wait()
                loads[3].wait()
                waited = 4

        def pack(kind, rows, lanes, relay, item, c=c):
            held_rows = (keys, values)[kind]
            outgoing[c][relay, item] = jnp.where(leaving == 1, held_rows[1, rows, lanes], held_rows[0, rows, lanes])

        copy_units(chunk, pack)
        if c == 0:
            pl.semaphore_wait(barrier, len(peers))
        if not slots[c]:
            sent_along[c] = send(outgoing[c], final[c], (partner, tensor), along_send.at[c], along_recv.at[c])
            continue
        depth = chunk[1] - chunk[0]
        for k in range(1, K):
            dx, dy = OFFSETS[k]
            send(
                outgoing[c].at[k], held[c].at[k * depth : (k + 1) * depth],
                (replica_at(plane, x + dx, y + dy), tensor), out_send.at[c], out_recv.at[c],
            )
        for item in range(depth):
            held[c][item] = outgoing[c][0, item]
    if waited == 2:
        loads[2].wait()
        loads[3].wait()

    if spread:
        leave_items = [items_of(replica_at(plane, x - dx, y - dy), k) for k, (dx, dy) in enumerate(OFFSETS)]
        come_items = [items_of(replica_at((plane + 2) % 4, x - dx, y - dy), k) for k, (dx, dy) in enumerate(OFFSETS)]

    def along(c):
        low, high = chunks[c]
        depth = high - low
        landing(held[c].at[depth:], out_recv.at[c]).wait_recv()
        ends, gaps, total = [], [], 0
        for items in leave_items:
            live = jnp.clip(items - low, 0, depth)
            total = total + live
            ends.append(total)
            gaps.append(depth - live)

        def step(group, carry):
            for lane in range(4):
                slot = jnp.minimum(group * 4 + lane, slots[c] - 1)
                place = slot
                for end, gap in zip(ends[:-1], gaps[:-1]):
                    place = place + jnp.where(slot >= end, gap, 0)
                packed[c][slot] = held[c][jnp.minimum(place, K * depth - 1)]
            return carry

        lax.fori_loop(0, -(-slots[c] // 4), step, 0)
        sent_along[c] = send(packed[c], unpacked[c], (partner, tensor), along_send.at[c], along_recv.at[c])

    def spread_back(c):
        sent_along[c].wait_recv()
        low, high = chunks[c]
        starts, total = [], 0
        for items in come_items:
            starts.append(total)
            total = total + jnp.clip(items - low, 0, high - low)
        for k in range(K - 1, -1, -1):
            target = final[c] if k == 0 else back[c]
            for item in range(high - low):
                target[k, item] = unpacked[c][jnp.minimum(starts[k] + item, slots[c] - 1)]
            if k:
                dx, dy = OFFSETS[k]
                send(
                    back[c].at[k], final[c].at[k], (replica_at(plane, x - dx, y - dy), tensor),
                    back_send.at[c], back_recv.at[c],
                )

    query_rows = queries[...].astype(jnp.float32)
    key_rows = new_key[...].astype(jnp.float32)
    value_rows = new_value[...].astype(jnp.float32)
    fresh_out[0:8] = as_rows(key_rows)
    fresh_out[8:16] = as_rows(value_rows)
    shares = []

    def attend():
        attended = []
        for slot in range(2):
            attended.append(
                attend_row(
                    query_rows[slot : slot + 1], key_rows[slot : slot + 1], value_rows[slot : slot + 1],
                    keys.at[slot], values.at[slot], lengths[replica * 2 + slot],
                )
            )
        attended = jnp.concatenate(attended + [jnp.zeros((6, attended[0].shape[1]), jnp.float32)], axis=0)
        attended = attended.astype(jnp.bfloat16)

        loads[4].wait()
        for piece in range(4):
            product = jnp.dot(
                attended, weights[:, piece * 1024 : (piece + 1) * 1024], preferred_element_type=jnp.float32
            )
            partial[piece] = as_rows(product[0:2])
        residual = hidden[:, pl.ds(pl.multiple_of(tensor * 1024, 1024), 1024)].astype(jnp.float32)
        partial[tensor] = partial[tensor] + as_rows(residual)

        shares.append(send(fresh_out, fresh_in, (partner, tensor), part_send.at[0], part_recv.at[0]))
        for k in range(1, 8):
            piece = (tensor + k) % 4
            shares.append(
                send(
                    partial.at[piece], partial_in.at[k], ((replica, partner)[k // 4], piece),
                    part_send.at[k], part_recv.at[k],
                )
            )

    def settle():
        for slot in range(2):
            length = jnp.where(leaving == slot, -1, lengths[replica * 2 + slot])
            for held_rows, fresh_rows in ((keys, key_rows), (values, value_rows)):
                fresh = jnp.broadcast_to(fresh_rows[slot : slot + 1], (TILE, fresh_rows.shape[1]))

                def step(block, carry, slot=slot, length=length, held_rows=held_rows, fresh=fresh):
                    rows = pl.ds(pl.multiple_of(block * TILE, TILE), TILE)
                    position = in_block + block * TILE
                    tile = held_rows[slot, rows, :].astype(jnp.float32)
                    tile = jnp.where(position < length, tile, jnp.where(position == length, fresh, 0.0))
                    held_rows[slot, rows, :] = tile.astype(jnp.bfloat16)
                    return carry

                lax.fori_loop(0, keys.shape[1] // TILE, step, 0)

    stores = []

    def store(rows, first_sem):
        for slot in range(2):
            for kind in range(2):
                copy = pltpu.make_async_copy(
                    (keys, values)[kind].at[slot, rows], settled.at[slot, kind, rows],
                    store_sem.at[first_sem + slot * 2 + kind],
                )
                copy.start()
                stores.append(copy)

    def finish():
        for share in shares:
            share.wait()
        here = partial[tensor] + partial_in[1] + partial_in[2] + partial_in[3]
        there = partial_in[4] + partial_in[5] + partial_in[6] + partial_in[7]
        coming = jnp.where(moved[partner] == 1, there[8:16], there[0:8])
        for slot in range(2):
            small_out[slot * 8 : slot * 8 + 8] = jnp.where(leaving == slot, coming, here[slot * 8 : slot * 8 + 8])
        for kind in range(2):
            first, second = fresh_in[kind * 8 : kind * 8 + 4], fresh_in[kind * 8 + 4 : kind * 8 + 8]
            come_fresh.append(as_line(jnp.where(moved[partner] == 1, second, first)))

    come_fresh = []
    come_length = lengths[partner * 2 + jnp.maximum(moved[partner], 0)]
    in_block = lax.broadcasted_iota(jnp.int32, (TILE, keys.shape[2]), 0)
    in_tile = lax.broadcasted_iota(jnp.int32, (TILE, LANES), 0)

    def land(c):
        chunk = chunks[c]
        if slots[c]:
            landing(final[c].at[1:], back_recv.at[c]).wait_recv()
        else:
            sent_along[c].wait_recv()

        def unpack(kind, rows, lanes, relay, item):
            position = in_tile + (item + chunk[0]) * (STEP * TILE) + relay // 4 * TILE
            fresh = jnp.broadcast_to(come_fresh[kind][:, lanes], (TILE, LANES))
            tile = final[c][relay, item].astype(jnp.float32)
            tile = jnp.where(position < come_length, tile, jnp.where(position == come_length, fresh, 0.0))
            tile = tile.astype(jnp.bfloat16)
            held_rows = (keys, values)[kind]
            for slot in range(2):
                held_rows[slot, rows, lanes] = jnp.where(leaving == slot, tile, held_rows[slot, rows, lanes])

        copy_units(chunk, unpack)
        store(slice(chunk[0] * STEP * TILE, chunk[1] * STEP * TILE), 4 * c)

    def settle_rest():
        settle()
        bottom = chunks[-1][1] * STEP * TILE
        if bottom < keys.shape[1]:
            store(slice(bottom, keys.shape[1]), 4 * count)

    steps = {"along": along, "attend": attend, "settle": settle_rest, "finish": finish, "back": spread_back, "land": land}
    for step, *chunk in ORDER if spread else PLAIN:
        steps[step](*chunk)
    for copy in sent_along.values():
        copy.wait_send()
    for c in spread:
        landing(outgoing[c].at[1:], out_send.at[c]).wait_send()
        landing(back[c].at[1:], back_send.at[c]).wait_send()
    for copy in stores:
        copy.wait()


def move(chunks, slots, collective_id, *operands):
    cache_keys, w_out = operands[6], operands[8]
    here, cap, width = cache_keys.shape
    count = len(chunks)
    any_spec = pl.BlockSpec(memory_space=pl.ANY)
    vmem_spec = pl.BlockSpec(memory_space=pltpu.VMEM)
    smem_spec = pl.BlockSpec(memory_space=pltpu.SMEM)

    def items(chunk):
        return pltpu.VMEM((K, chunk[1] - chunk[0], TILE, LANES), jnp.bfloat16)

    buffers = [items(chunk) for chunk in chunks] * 2
    for chunk, size in zip(chunks, slots):
        if size:
            on_the_way = pltpu.VMEM((size, TILE, LANES), jnp.bfloat16)
            flat = pltpu.VMEM((K * (chunk[1] - chunk[0]), TILE, LANES), jnp.bfloat16)
            buffers += [flat, on_the_way, on_the_way, items(chunk)]
    return pl.pallas_call(
        functools.partial(move_kernel, chunks, slots),
        out_shape=(
            jax.ShapeDtypeStruct((16, 128), jnp.float32),
            jax.ShapeDtypeStruct((here, 2, cap, width), jnp.bfloat16),
        ),
        in_specs=[smem_spec] * 2 + [vmem_spec] * 4 + [any_spec] * 3,
        out_specs=(vmem_spec, any_spec),
        scratch_shapes=[
            pltpu.VMEM((here, cap, width), jnp.bfloat16),
            pltpu.VMEM((here, cap, width), jnp.bfloat16),
            pltpu.VMEM(w_out.shape, jnp.bfloat16),
            pltpu.VMEM((4, 16, 128), jnp.float32),
            pltpu.VMEM((8, 16, 128), jnp.float32),
            pltpu.VMEM((16, 128), jnp.float32),
            pltpu.VMEM((16, 128), jnp.float32),
            pltpu.SemaphoreType.DMA((5,)),
            pltpu.SemaphoreType.DMA((8,)),
            pltpu.SemaphoreType.DMA((8,)),
            pltpu.SemaphoreType.DMA((count,)),
            pltpu.SemaphoreType.DMA((count,)),
            pltpu.SemaphoreType.DMA((count,)),
            pltpu.SemaphoreType.DMA((count,)),
            pltpu.SemaphoreType.DMA((count,)),
            pltpu.SemaphoreType.DMA((count,)),
            pltpu.SemaphoreType.DMA((4 * count + 4,)),
            *buffers,
        ],
        compiler_params=pltpu.CompilerParams(
            collective_id=collective_id, has_side_effects=True, vmem_limit_bytes=56 * 2**20
        ),
        name="move%d" % collective_id,
    )(*operands)


def place_kernel(small, settled, layer_out, keys_out, values_out, sems):
    copies = []
    for slot in range(2):
        for kind, target in enumerate((keys_out, values_out)):
            copy = pltpu.make_async_copy(settled.at[slot, kind], target.at[slot], sems.at[slot * 2 + kind])
            copy.start()
            copies.append(copy)
    layer_out[...] = jnp.concatenate([as_line(small[0:8]), as_line(small[8:16])], axis=0).astype(jnp.bfloat16)
    for copy in copies:
        copy.wait()


def choose_kernel(lengths, moved, choice):
    row = lax.broadcasted_iota(jnp.int32, (64, 64), 0)
    col = lax.broadcasted_iota(jnp.int32, (64, 64), 1)
    slot = jnp.sum(jnp.where(row == col, moved[...].astype(jnp.float32), 0.0), axis=1, keepdims=True)
    moves = slot >= 0.0
    wide_row = lax.broadcasted_iota(jnp.int32, (64, 128), 0)
    wide_col = lax.broadcasted_iota(jnp.int32, (64, 128), 1)
    wanted = wide_col.astype(jnp.float32) == 2.0 * wide_row.astype(jnp.float32) + jnp.maximum(slot, 0.0)
    length = jnp.sum(jnp.where(wanted, lengths[...].astype(jnp.float32), 0.0), axis=1, keepdims=True)
    blocks = jnp.where(moves, jnp.floor((length + TILE) * (1.0 / TILE)), 0.0)
    longest = jnp.max(blocks).astype(jnp.int32)
    relays = []
    for first in range(STEP):
        some = row < 0
        for dx, dy in OFFSETS[first * 4 : first * 4 + 4]:
            there = (row & 48) + ((((row >> 2) + dx) & 3) << 2) + ((row + dy) & 3)
            some = some | (there == col)
        relays.append((some, jnp.floor((blocks + (STEP - 1 - first)) * (1.0 / STEP))))
    needs = []
    for low, high in CHUNKS[1:]:
        load = 0.0
        for some, items in relays:
            live = jnp.clip(items - low, 0.0, float(high - low))
            load = load + jnp.where(some, live, 0.0)
        needs.append(jnp.max(jnp.sum(load, axis=0)).astype(jnp.int32))
    result = 0
    for level in LEVELS:
        fits = longest <= SHORT
        for need, size in zip(needs, level[1:]):
            fits = fits & (need <= size)
        result = result + jnp.where(fits, 0, 1)
    choice[0] = result + jnp.where(longest <= SHORT, 0, 1)


def shards(
    hidden, queries, new_key, new_value, cache_keys, cache_values, w_out, lengths, moved_slot
):
    slots, cap, width = cache_keys.shape
    any_spec = pl.BlockSpec(memory_space=pl.ANY)
    vmem_spec = pl.BlockSpec(memory_space=pltpu.VMEM)
    smem_spec = pl.BlockSpec(memory_space=pltpu.SMEM)

    choice = pl.pallas_call(
        choose_kernel,
        out_shape=jax.ShapeDtypeStruct((1,), jnp.int32),
        in_specs=[vmem_spec] * 2,
        out_specs=smem_spec,
        name="choose",
    )(lengths.reshape(1, -1), moved_slot.reshape(1, -1))

    builds = [functools.partial(move, CHUNKS, level, i) for i, level in enumerate(LEVELS)]
    builds.append(functools.partial(move, CHUNKS, DIRECT, len(builds)))
    builds.append(functools.partial(move, WHOLE, DIRECT, len(builds)))
    small, settled = lax.switch(
        choice[0], builds,
        lengths, moved_slot, hidden, queries, new_key, new_value, cache_keys, cache_values, w_out,
    )

    return pl.pallas_call(
        place_kernel,
        out_shape=(
            jax.ShapeDtypeStruct((slots, w_out.shape[1] // 4), jnp.bfloat16),
            jax.ShapeDtypeStruct(cache_keys.shape, cache_keys.dtype),
            jax.ShapeDtypeStruct(cache_keys.shape, cache_keys.dtype),
        ),
        in_specs=[vmem_spec, any_spec],
        out_specs=(vmem_spec, any_spec, any_spec),
        scratch_shapes=[pltpu.SemaphoreType.DMA((4,))],
        name="place",
    )(small, settled)


def solution(mesh):
    return jax.shard_map(
        shards,
        mesh=mesh,
        in_specs=(
            P("replica", None),
            P("replica", "tensor"),
            P("replica", "tensor"),
            P("replica", "tensor"),
            P("replica", None, "tensor"),
            P("replica", None, "tensor"),
            P("tensor", None),
            P(),
            P(),
        ),
        out_specs=(
            P("replica", "tensor"),
            P("replica", None, "tensor"),
            P("replica", None, "tensor"),
        ),
        check_vma=False,
    )
```

```python
import functools

import jax
import jax.numpy as jnp
from jax import lax
from jax.experimental import pallas as pl
from jax.experimental.pallas import tpu as pltpu
from jax.sharding import PartitionSpec as P

HEAD_DIM = 128
TILE = 16
LANES = 256
MESH = pl.DeviceIdType.MESH

OFFSETS = tuple((dx, dy) for dx in range(4) for dy in range(4))
K = len(OFFSETS)
STEP = K // 4
SHORT = 36
CHUNKS = ((0, 1), (1, 4), (4, 6), (6, 9))
LEVELS = ((0, 23, 12, 12), (0, 25, 14, 14), (0, 28, 15, 15), (0, 31, 17, 17), (0, 34, 18, 18))
DIRECT = (0, 0, 0, 0)
WHOLE = ((0, 3), (3, 6), (6, 9), (9, 12))
ORDER = (
    ("attend",), ("along", 1), ("settle",), ("back", 1), ("along", 2), ("finish",), ("land", 0),
    ("back", 2), ("along", 3), ("land", 1), ("back", 3), ("land", 2), ("land", 3),
)
PLAIN = (("attend",), ("settle",), ("finish",), ("land", 0), ("land", 1), ("land", 2), ("land", 3))
SPLIT = 256


def block_diagonal(row, heads):
    width = row.shape[1]
    row_id = lax.broadcasted_iota(jnp.int32, (8, width), 0)
    col_id = lax.broadcasted_iota(jnp.int32, (8, width), 1)
    own = (col_id >= row_id * HEAD_DIM) & (col_id < row_id * HEAD_DIM + HEAD_DIM)
    return own, jnp.where(own, jnp.broadcast_to(row, (8, width)), 0.0)


def attend_row(query, fresh_key, fresh_value, keys_ref, values_ref, length):
    width = keys_ref.shape[1]
    own, query_block = block_diagonal(query, width // HEAD_DIM)
    scale = HEAD_DIM**-0.5
    scores = lax.dot_general(
        query_block.astype(jnp.bfloat16), keys_ref[...], (((1,), (1,)), ((), ())), preferred_element_type=jnp.float32
    )
    scores = scores * scale
    fresh_score = jnp.sum(query_block * fresh_key, axis=1, keepdims=True) * scale
    position = lax.broadcasted_iota(jnp.int32, scores.shape, 1)
    live = position < length
    peak = jnp.maximum(jnp.max(jnp.where(live, scores, -1e30), axis=1, keepdims=True), fresh_score)
    terms = jnp.where(live, jnp.exp(jnp.minimum(scores - peak, 0.0)), 0.0)
    fresh_term = jnp.exp(fresh_score - peak)
    total = jnp.sum(terms, axis=1, keepdims=True) + fresh_term
    weights = (terms / total).astype(jnp.bfloat16)
    fresh_weight = (fresh_term / total).astype(jnp.bfloat16).astype(jnp.float32)
    mixed = lax.dot_general(
        weights, values_ref[...], (((1,), (0,)), ((), ())), preferred_element_type=jnp.float32
    )
    mixed = mixed + fresh_weight * fresh_value
    return jnp.sum(jnp.where(own, mixed, 0.0), axis=0, keepdims=True)


def as_rows(two_rows):
    count = two_rows.shape[1] // 128
    pieces = [two_rows[s : s + 1, j * 128 : (j + 1) * 128] for s in range(2) for j in range(count)]
    return jnp.concatenate(pieces, axis=0)


def as_line(rows):
    return jnp.concatenate([rows[j : j + 1, :] for j in range(rows.shape[0])], axis=1)


def replica_at(plane, x, y):
    return plane * 16 + (x % 4) * 4 + y % 4


def move_kernel(
    chunks, slots,
    lengths, moved, hidden, queries, new_key, new_value, cache_keys, cache_values, w_out,
    small_out, settled,
    keys, values, weights, partial, partial_in, fresh_out, fresh_in,
    load_sem, part_send, part_recv, along_send, along_recv, out_send, out_recv, back_send, back_recv, store_sem,
    *buffers,
):
    count = len(chunks)
    outgoing, buffers = buffers[:count], buffers[count:]
    final, buffers = buffers[:count], buffers[count:]
    held, packed, unpacked, back = {}, {}, {}, {}
    spread = [c for c in range(count) if slots[c]]
    for i, c in enumerate(spread):
        held[c], packed[c], unpacked[c], back[c] = buffers[i * 4 : i * 4 + 4]
    replica = lax.axis_index("replica")
    tensor = lax.axis_index("tensor")
    plane, x, y = replica // 16, (replica // 4) % 4, replica % 4
    partner = (replica + 32) % 64

    loads = []
    parts = [(cache, held_rows, span) for span in (slice(0, SPLIT), slice(SPLIT, None)) for cache, held_rows in ((cache_keys, keys), (cache_values, values))]
    for i, (cache, held_rows, span) in enumerate(parts):
        loads.append(pltpu.make_async_copy(cache.at[:, span], held_rows.at[:, span], load_sem.at[i]))
    loads.append(pltpu.make_async_copy(w_out, weights, load_sem.at[4]))
    for load in loads:
        load.start()

    peers = [(replica, (tensor + k) % 4) for k in range(1, 4)]
    peers += [(partner, (tensor + k) % 4) for k in range(4)]
    if spread:
        peers += [(replica_at(plane, x + dx, y + dy), tensor) for dx, dy in OFFSETS[1:]]
    barrier = pltpu.get_barrier_semaphore()
    for peer in peers:
        pl.semaphore_signal(barrier, inc=1, device_id=peer, device_id_type=MESH)

    leaving = moved[replica]

    def items_of(source, k):
        slot = moved[source]
        length = lengths[source * 2 + jnp.maximum(slot, 0)]
        return jnp.where(slot >= 0, ((length + TILE) >> 4) + (STEP - 1 - k // 4) >> (STEP.bit_length() - 1), 0)

    def send(source, target, device, send_sem, recv_sem):
        copy = pltpu.make_async_remote_copy(
            src_ref=source, dst_ref=target, send_sem=send_sem, recv_sem=recv_sem,
            device_id=device, device_id_type=MESH,
        )
        copy.start()
        return copy

    def landing(buffer, sem):
        return pltpu.make_async_remote_copy(
            src_ref=buffer, dst_ref=buffer, send_sem=sem, recv_sem=sem, device_id=(partner, tensor), device_id_type=MESH
        )

    def copy_units(chunk, body):
        def step(item, carry):
            for k in range(K):
                rows = pl.ds(pl.multiple_of((item * STEP + k // 4) * TILE, TILE), TILE)
                lanes = slice(k % 2 * LANES, (k % 2 + 1) * LANES)
                body(k % 4 // 2, rows, lanes, k, item - chunk[0])
            return carry

        lax.fori_loop(chunk[0], chunk[1], step, 0)

    waited = 0
    sent_along = {}
    for c, chunk in enumerate(chunks):
        if c == 0 or (waited == 2 and chunk[1] * STEP * TILE > SPLIT):
            loads[waited].wait()
            loads[waited + 1].wait()
            waited += 2
            if chunk[1] * STEP * TILE > SPLIT and waited == 2:
                loads[2].wait()
                loads[3].wait()
                waited = 4

        def pack(kind, rows, lanes, relay, item, c=c):
            held_rows = (keys, values)[kind]
            outgoing[c][relay, item] = jnp.where(leaving == 1, held_rows[1, rows, lanes], held_rows[0, rows, lanes])

        copy_units(chunk, pack)
        if c == 0:
            pl.semaphore_wait(barrier, len(peers))
        if not slots[c]:
            sent_along[c] = send(outgoing[c], final[c], (partner, tensor), along_send.at[c], along_recv.at[c])
            continue
        depth = chunk[1] - chunk[0]
        for k in range(1, K):
            dx, dy = OFFSETS[k]
            send(
                outgoing[c].at[k], held[c].at[k * depth : (k + 1) * depth],
                (replica_at(plane, x + dx, y + dy), tensor), out_send.at[c], out_recv.at[c],
            )
        for item in range(depth):
            held[c][item] = outgoing[c][0, item]
    if waited == 2:
        loads[2].wait()
        loads[3].wait()

    if spread:
        leave_items = [items_of(replica_at(plane, x - dx, y - dy), k) for k, (dx, dy) in enumerate(OFFSETS)]
        come_items = [items_of(replica_at((plane + 2) % 4, x - dx, y - dy), k) for k, (dx, dy) in enumerate(OFFSETS)]

    def along(c):
        low, high = chunks[c]
        depth = high - low
        landing(held[c].at[depth:], out_recv.at[c]).wait_recv()
        ends, gaps, total = [], [], 0
        for items in leave_items:
            live = jnp.clip(items - low, 0, depth)
            total = total + live
            ends.append(total)
            gaps.append(depth - live)

        def step(group, carry):
            for lane in range(4):
                slot = jnp.minimum(group * 4 + lane, slots[c] - 1)
                place = slot
                for end, gap in zip(ends[:-1], gaps[:-1]):
                    place = place + jnp.where(slot >= end, gap, 0)
                packed[c][slot] = held[c][jnp.minimum(place, K * depth - 1)]
            return carry

        lax.fori_loop(0, -(-slots[c] // 4), step, 0)
        sent_along[c] = send(packed[c], unpacked[c], (partner, tensor), along_send.at[c], along_recv.at[c])

    def spread_back(c):
        sent_along[c].wait_recv()
        low, high = chunks[c]
        starts, total = [], 0
        for items in come_items:
            starts.append(total)
            total = total + jnp.clip(items - low, 0, high - low)
        for k in range(K - 1, -1, -1):
            target = final[c] if k == 0 else back[c]
            for item in range(high - low):
                target[k, item] = unpacked[c][jnp.minimum(starts[k] + item, slots[c] - 1)]
            if k:
                dx, dy = OFFSETS[k]
                send(
                    back[c].at[k], final[c].at[k], (replica_at(plane, x - dx, y - dy), tensor),
                    back_send.at[c], back_recv.at[c],
                )

    query_rows = queries[...].astype(jnp.float32)
    key_rows = new_key[...].astype(jnp.float32)
    value_rows = new_value[...].astype(jnp.float32)
    fresh_out[0:8] = as_rows(key_rows)
    fresh_out[8:16] = as_rows(value_rows)
    shares = []

    def attend():
        attended = []
        for slot in range(2):
            attended.append(
                attend_row(
                    query_rows[slot : slot + 1], key_rows[slot : slot + 1], value_rows[slot : slot + 1],
                    keys.at[slot], values.at[slot], lengths[replica * 2 + slot],
                )
            )
        attended = jnp.concatenate(attended + [jnp.zeros((6, attended[0].shape[1]), jnp.float32)], axis=0)
        attended = attended.astype(jnp.bfloat16)

        loads[4].wait()
        for piece in range(4):
            product = jnp.dot(
                attended, weights[:, piece * 1024 : (piece + 1) * 1024], preferred_element_type=jnp.float32
            )
            partial[piece] = as_rows(product[0:2])
        residual = hidden[:, pl.ds(pl.multiple_of(tensor * 1024, 1024), 1024)].astype(jnp.float32)
        partial[tensor] = partial[tensor] + as_rows(residual)

        shares.append(send(fresh_out, fresh_in, (partner, tensor), part_send.at[0], part_recv.at[0]))
        for k in range(1, 8):
            piece = (tensor + k) % 4
            shares.append(
                send(
                    partial.at[piece], partial_in.at[k], ((replica, partner)[k // 4], piece),
                    part_send.at[k], part_recv.at[k],
                )
            )

    def settle():
        for slot in range(2):
            length = jnp.where(leaving == slot, -1, lengths[replica * 2 + slot])
            for held_rows, fresh_rows in ((keys, key_rows), (values, value_rows)):
                fresh = jnp.broadcast_to(fresh_rows[slot : slot + 1], (TILE, fresh_rows.shape[1]))

                def step(block, carry, slot=slot, length=length, held_rows=held_rows, fresh=fresh):
                    rows = pl.ds(pl.multiple_of(block * TILE, TILE), TILE)
                    position = in_block + block * TILE
                    tile = held_rows[slot, rows, :].astype(jnp.float32)
                    tile = jnp.where(position < length, tile, jnp.where(position == length, fresh, 0.0))
                    held_rows[slot, rows, :] = tile.astype(jnp.bfloat16)
                    return carry

                lax.fori_loop(0, keys.shape[1] // TILE, step, 0)

    stores = []

    def store(rows, first_sem):
        for slot in range(2):
            for kind in range(2):
                copy = pltpu.make_async_copy(
                    (keys, values)[kind].at[slot, rows], settled.at[slot, kind, rows],
                    store_sem.at[first_sem + slot * 2 + kind],
                )
                copy.start()
                stores.append(copy)

    def finish():
        for share in shares:
            share.wait()
        here = partial[tensor] + partial_in[1] + partial_in[2] + partial_in[3]
        there = partial_in[4] + partial_in[5] + partial_in[6] + partial_in[7]
        coming = jnp.where(moved[partner] == 1, there[8:16], there[0:8])
        for slot in range(2):
            small_out[slot * 8 : slot * 8 + 8] = jnp.where(leaving == slot, coming, here[slot * 8 : slot * 8 + 8])
        for kind in range(2):
            first, second = fresh_in[kind * 8 : kind * 8 + 4], fresh_in[kind * 8 + 4 : kind * 8 + 8]
            come_fresh.append(as_line(jnp.where(moved[partner] == 1, second, first)))

    come_fresh = []
    come_length = lengths[partner * 2 + jnp.maximum(moved[partner], 0)]
    in_block = lax.broadcasted_iota(jnp.int32, (TILE, keys.shape[2]), 0)
    in_tile = lax.broadcasted_iota(jnp.int32, (TILE, LANES), 0)

    def land(c):
        chunk = chunks[c]
        if slots[c]:
            landing(final[c].at[1:], back_recv.at[c]).wait_recv()
        else:
            sent_along[c].wait_recv()

        def unpack(kind, rows, lanes, relay, item):
            position = in_tile + (item + chunk[0]) * (STEP * TILE) + relay // 4 * TILE
            fresh = jnp.broadcast_to(come_fresh[kind][:, lanes], (TILE, LANES))
            tile = final[c][relay, item].astype(jnp.float32)
            tile = jnp.where(position < come_length, tile, jnp.where(position == come_length, fresh, 0.0))
            tile = tile.astype(jnp.bfloat16)
            held_rows = (keys, values)[kind]
            for slot in range(2):
                held_rows[slot, rows, lanes] = jnp.where(leaving == slot, tile, held_rows[slot, rows, lanes])

        copy_units(chunk, unpack)
        store(slice(chunk[0] * STEP * TILE, chunk[1] * STEP * TILE), 4 * c)

    def settle_rest():
        settle()
        bottom = chunks[-1][1] * STEP * TILE
        if bottom < keys.shape[1]:
            store(slice(bottom, keys.shape[1]), 4 * count)

    steps = {"along": along, "attend": attend, "settle": settle_rest, "finish": finish, "back": spread_back, "land": land}
    for step, *chunk in ORDER if spread else PLAIN:
        steps[step](*chunk)
    for copy in sent_along.values():
        copy.wait_send()
    for c in spread:
        landing(outgoing[c].at[1:], out_send.at[c]).wait_send()
        landing(back[c].at[1:], back_send.at[c]).wait_send()
    for copy in stores:
        copy.wait()


def move(chunks, slots, collective_id, *operands):
    cache_keys, w_out = operands[6], operands[8]
    here, cap, width = cache_keys.shape
    count = len(chunks)
    any_spec = pl.BlockSpec(memory_space=pl.ANY)
    vmem_spec = pl.BlockSpec(memory_space=pltpu.VMEM)
    smem_spec = pl.BlockSpec(memory_space=pltpu.SMEM)

    def items(chunk):
        return pltpu.VMEM((K, chunk[1] - chunk[0], TILE, LANES), jnp.bfloat16)

    buffers = [items(chunk) for chunk in chunks] * 2
    for chunk, size in zip(chunks, slots):
        if size:
            on_the_way = pltpu.VMEM((size, TILE, LANES), jnp.bfloat16)
            flat = pltpu.VMEM((K * (chunk[1] - chunk[0]), TILE, LANES), jnp.bfloat16)
            buffers += [flat, on_the_way, on_the_way, items(chunk)]
    return pl.pallas_call(
        functools.partial(move_kernel, chunks, slots),
        out_shape=(
            jax.ShapeDtypeStruct((16, 128), jnp.float32),
            jax.ShapeDtypeStruct((here, 2, cap, width), jnp.bfloat16),
        ),
        in_specs=[smem_spec] * 2 + [vmem_spec] * 4 + [any_spec] * 3,
        out_specs=(vmem_spec, any_spec),
        scratch_shapes=[
            pltpu.VMEM((here, cap, width), jnp.bfloat16),
            pltpu.VMEM((here, cap, width), jnp.bfloat16),
            pltpu.VMEM(w_out.shape, jnp.bfloat16),
            pltpu.VMEM((4, 16, 128), jnp.float32),
            pltpu.VMEM((8, 16, 128), jnp.float32),
            pltpu.VMEM((16, 128), jnp.float32),
            pltpu.VMEM((16, 128), jnp.float32),
            pltpu.SemaphoreType.DMA((5,)),
            pltpu.SemaphoreType.DMA((8,)),
            pltpu.SemaphoreType.DMA((8,)),
            pltpu.SemaphoreType.DMA((count,)),
            pltpu.SemaphoreType.DMA((count,)),
            pltpu.SemaphoreType.DMA((count,)),
            pltpu.SemaphoreType.DMA((count,)),
            pltpu.SemaphoreType.DMA((count,)),
            pltpu.SemaphoreType.DMA((count,)),
            pltpu.SemaphoreType.DMA((4 * count + 4,)),
            *buffers,
        ],
        compiler_params=pltpu.CompilerParams(
            collective_id=collective_id, has_side_effects=True, vmem_limit_bytes=56 * 2**20
        ),
        name="move%d" % collective_id,
    )(*operands)


def place_kernel(small, settled, layer_out, keys_out, values_out, sems):
    copies = []
    for slot in range(2):
        for kind, target in enumerate((keys_out, values_out)):
            copy = pltpu.make_async_copy(settled.at[slot, kind], target.at[slot], sems.at[slot * 2 + kind])
            copy.start()
            copies.append(copy)
    layer_out[...] = jnp.concatenate([as_line(small[0:8]), as_line(small[8:16])], axis=0).astype(jnp.bfloat16)
    for copy in copies:
        copy.wait()


def choose_kernel(lengths, moved, choice):
    row = lax.broadcasted_iota(jnp.int32, (64, 64), 0)
    col = lax.broadcasted_iota(jnp.int32, (64, 64), 1)
    slot = jnp.sum(jnp.where(row == col, moved[...].astype(jnp.float32), 0.0), axis=1, keepdims=True)
    moves = slot >= 0.0
    wide_row = lax.broadcasted_iota(jnp.int32, (64, 128), 0)
    wide_col = lax.broadcasted_iota(jnp.int32, (64, 128), 1)
    wanted = wide_col.astype(jnp.float32) == 2.0 * wide_row.astype(jnp.float32) + jnp.maximum(slot, 0.0)
    length = jnp.sum(jnp.where(wanted, lengths[...].astype(jnp.float32), 0.0), axis=1, keepdims=True)
    blocks = jnp.where(moves, jnp.floor((length + TILE) * (1.0 / TILE)), 0.0)
    longest = jnp.max(blocks).astype(jnp.int32)
    relays = []
    for first in range(STEP):
        some = row < 0
        for dx, dy in OFFSETS[first * 4 : first * 4 + 4]:
            there = (row & 48) + ((((row >> 2) + dx) & 3) << 2) + ((row + dy) & 3)
            some = some | (there == col)
        relays.append((some, jnp.floor((blocks + (STEP - 1 - first)) * (1.0 / STEP))))
    needs = []
    for low, high in CHUNKS[1:]:
        load = 0.0
        for some, items in relays:
            live = jnp.clip(items - low, 0.0, float(high - low))
            load = load + jnp.where(some, live, 0.0)
        needs.append(jnp.max(jnp.sum(load, axis=0)).astype(jnp.int32))
    result = 0
    for level in LEVELS:
        fits = longest <= SHORT
        for need, size in zip(needs, level[1:]):
            fits = fits & (need <= size)
        result = result + jnp.where(fits, 0, 1)
    choice[0] = result + jnp.where(longest <= SHORT, 0, 1)


def shards(
    hidden, queries, new_key, new_value, cache_keys, cache_values, w_out, lengths, moved_slot
):
    slots, cap, width = cache_keys.shape
    any_spec = pl.BlockSpec(memory_space=pl.ANY)
    vmem_spec = pl.BlockSpec(memory_space=pltpu.VMEM)
    smem_spec = pl.BlockSpec(memory_space=pltpu.SMEM)

    choice = pl.pallas_call(
        choose_kernel,
        out_shape=jax.ShapeDtypeStruct((1,), jnp.int32),
        in_specs=[vmem_spec] * 2,
        out_specs=smem_spec,
        name="choose",
    )(lengths.reshape(1, -1), moved_slot.reshape(1, -1))

    builds = [functools.partial(move, CHUNKS, level, i) for i, level in enumerate(LEVELS)]
    builds.append(functools.partial(move, CHUNKS, DIRECT, len(builds)))
    builds.append(functools.partial(move, WHOLE, DIRECT, len(builds)))
    small, settled = lax.switch(
        choice[0], builds,
        lengths, moved_slot, hidden, queries, new_key, new_value, cache_keys, cache_values, w_out,
    )

    return pl.pallas_call(
        place_kernel,
        out_shape=(
            jax.ShapeDtypeStruct((slots, w_out.shape[1] // 4), jnp.bfloat16),
            jax.ShapeDtypeStruct(cache_keys.shape, cache_keys.dtype),
            jax.ShapeDtypeStruct(cache_keys.shape, cache_keys.dtype),
        ),
        in_specs=[vmem_spec, any_spec],
        out_specs=(vmem_spec, any_spec, any_spec),
        scratch_shapes=[pltpu.SemaphoreType.DMA((4,))],
        name="place",
    )(small, settled)


def solution(mesh):
    return jax.shard_map(
        shards,
        mesh=mesh,
        in_specs=(
            P("replica", None),
            P("replica", "tensor"),
            P("replica", "tensor"),
            P("replica", "tensor"),
            P("replica", None, "tensor"),
            P("replica", None, "tensor"),
            P("tensor", None),
            P(),
            P(),
        ),
        out_specs=(
            P("replica", "tensor"),
            P("replica", None, "tensor"),
            P("replica", None, "tensor"),
        ),
        check_vma=False,
    )
```
